128 devices in a mesh: expert: 16 (over z, y), tensor: 8 (over x, core).
Axes of the slice: x: 4, y: 4, z: 4, core: 2. Of those that a mesh axis runs over, the one named last changes fastest.
Arguments:
- context: bfloat16 [16384, 4096], P('expert', 'tensor'), may hold values from -6 to 6
- out_proj: bfloat16 [4096, 2880], P('tensor'), may hold values from -0.09375 to 0.09375
- residual_in: bfloat16 [16384, 2880], P(('expert', 'tensor')), may hold values from -36 to 36
- gain: bfloat16 [2880], replicated, may hold values from 0.099609375 to 1.8984375
- up_weight: bfloat16 [128, 2880, 1440], P(('expert', 'tensor')), may hold values from -0.109375 to 0.109375
- down_weight: bfloat16 [128, 1440, 2880], P(('expert', 'tensor')), may hold values from -0.15625 to 0.15625
- expert_ids: int32 [16384, 4], P(('expert', 'tensor')), may hold values from 0 to 127, all different within a row; in each aligned block of 128 rows (0 to 127, 128 to 255, ...) at most 5 rows name the same one
- gate_counts: int32 [16384, 4], P(('expert', 'tensor')), may hold values from 1 to 8
- grad_out: bfloat16 [16384, 2880], P(('expert', 'tensor')), may hold values from -6 to 6
Outputs:
- mixed: bfloat16 [16384, 2880], P(('expert', 'tensor'))
- grad_residual: bfloat16 [16384, 2880], P(('expert', 'tensor'))
- grad_context: bfloat16 [16384, 4096], P('expert', 'tensor')
The draws below stay inside these ranges and needn't reach their ends.
Inputs may be any that keep to these rules, and one draw needn't show every extreme that they name: `expert_ids`: each row names 4 different experts. Among the 128 rows of one device no expert is named more than 5 times, a bound that some block reaches.
All inputs are finite; a program needn't handle non-finite values.
Results may differ from the reference program's by a relative error of at most 0.011.
Values may be sent and summed in bfloat16 or wider, within the bound.
A program may use at most 192 MiB of HBM per device.

```python
import math
import jax
import jax.numpy as jnp
import numpy as np
from jax import lax

D = 2880
HEADS = 64
HD = 64
TOP = 4
FF = 1440
TOK_DEV = 128
TOKENS = 16384
EXPERTS = 128
CAP = 5
N_EXPERT = 16
N_TENSOR = 8


def draw_residual_in(key, part):
    key = jax.random.fold_in(key, 11)
    base_key, row_key, col_key = jax.random.split(key, 3)
    base_values = jax.random.truncated_normal(base_key, -4.0, 4.0, (TOKENS, D), jnp.float32)
    row_scale = jnp.exp(jax.random.uniform(row_key, (TOKENS, 1), jnp.float32, math.log(0.3), math.log(3.0)))
    col_scale = jnp.exp(jax.random.uniform(col_key, (1, D), jnp.float32, math.log(0.3), math.log(3.0)))
    return (base_values * row_scale * col_scale).astype(jnp.bfloat16)


def touch_ends(result, own_key, smallest, largest):
    longest = result.shape.index(max(result.shape))
    spots = []
    for shift in (0, 1):
        where = [jax.random.randint(jax.random.fold_in(own_key, axis), (), 0, length) for axis, length in enumerate(result.shape)]
        where[longest] = (where[longest] + shift) % result.shape[longest]
        spots.append(tuple(where))
    return result.at[spots[0]].set(smallest).at[spots[1]].set(largest)


def levels(stream_key, shape, shards, least, largest):
    level, own = 1.0, jax.random.fold_in(stream_key, 6)
    for axis_at, shards_of in shards:
        heights = jnp.exp(jax.random.uniform(jax.random.fold_in(own, axis_at), (shards_of,), jnp.float32, least / len(shards), largest / len(shards)))
        level = level * jnp.repeat(heights, shape[axis_at] // shards_of).reshape([-1 if axis == axis_at else 1 for axis in range(len(shape))])
    return level


def shared_out(key, own, number, rows, count, top, reach, lean):
    sequence = jax.random.permutation(key, count)
    heavy_load, common = shares(count, rows * top, reach, lean, True), shares(count, rows * top, reach, lean, False)
    places = jnp.arange(count)

    def named(sizes, offset_by):
        used = int((sizes > 0).sum())
        fixed = max(1, used // 4)
        passed = fixed + (places - fixed + offset_by * (used - fixed)) % max(1, count - fixed)
        return jnp.zeros((count,), jnp.int32).at[sequence[jnp.where(places < fixed, places, passed)]].set(jnp.asarray(sizes, jnp.int32))

    sizes = jnp.where(number % 4 == 0, named(heavy_load, number // 4), named(common, number - number // 4 - 1))
    mixed = jax.random.permutation(jax.random.fold_in(own, 3), count)
    giver, sink = mixed[0:count // 2 * 2:2], mixed[1:count // 2 * 2:2]
    room = jnp.minimum(sizes[giver] - 1, reach - sizes[sink]) // 2
    room = jnp.where((giver == sequence[0]) | (sink == sequence[0]) | (sizes[sink] == 0), 0, jnp.maximum(room, 0))
    passed = jax.random.randint(jax.random.fold_in(own, 4), (count // 2,), 0, 1 << 20) % (room + 1)
    sizes = sizes.at[giver].add(-passed).at[sink].add(passed)
    labels = jnp.searchsorted(jnp.cumsum(sizes), jnp.arange(rows * top), side="right").astype(jnp.int32)
    grid = labels.reshape(top, rows).T
    grid = grid[jax.random.permutation(jax.random.fold_in(own, 1), rows)]
    offset_by = jax.random.randint(jax.random.fold_in(own, 2), (rows, 1), 0, top)
    return jnp.take_along_axis(grid, (jnp.arange(top)[None, :] + offset_by) % top, axis=1)


def shares(number_of, total, bound, slope, full):
    portions = [(1 << 20) // math.isqrt(rank ** slope) + 1 for rank in range(1, number_of + 1)]
    largest = bound if full else min(bound, max(-(-total // number_of), total * portions[0] // sum(portions)))
    least = 1 if total - largest >= number_of - 1 else 0
    given, spare = [largest] + [least] * (number_of - 1), total - largest - least * (number_of - 1)
    while spare > 0:
        free = [i for i in range(1, number_of) if given[i] < largest] or [i for i in range(1, number_of) if given[i] < bound]
        pool, remaining = sum([portions[i] for i in free]), spare
        for i in free:
            addition = min(bound - given[i], max(1, remaining * portions[i] // pool), spare)
            given[i] = given[i] + addition
            spare = spare - addition
    return np.array(given)


def gaussian(key, extent, scale, limit, shards=(), kind=jnp.bfloat16):
    result = jax.random.normal(key, extent, jnp.float32) * scale
    if len(shards) > 0:
        result = levels(key, extent, shards, -0.22, 0.18) * result
    return jnp.clip(result, min=-limit, max=limit).astype(kind)


def setup_inputs(seed: int = 0) -> dict:
    keys = jax.random.split(jax.random.key(seed), 10)
    context = gaussian(keys[0], (TOKENS, HEADS * HD), 1.0, 6.0, ((0, 16), (1, 8)))
    out_proj = gaussian(keys[1], (HEADS * HD, D), (HEADS * HD) ** -0.5, 0.09375, ((0, 8),))
    residual_in = draw_residual_in(jax.random.fold_in(keys[9], 71), 0)
    gain = jnp.clip(1.0 + 0.18 * jax.random.normal(keys[3], (D,), jnp.float32), 0.099609375, 1.8984375).astype(jnp.bfloat16)
    up_weight = gaussian(keys[4], (EXPERTS, D, FF), D ** -0.5, 0.109375, ((0, 128),))
    down_weight = gaussian(keys[5], (EXPERTS, FF, D), FF ** -0.5, 0.15625, ((0, 128),))
    expert_ids_keys = jax.random.split(jax.random.fold_in(keys[6], 1), TOKENS // TOK_DEV)
    expert_ids_turns = jax.random.permutation(jax.random.fold_in(keys[6], 3), TOKENS // TOK_DEV)
    expert_ids = jax.vmap(lambda own, number: shared_out(jax.random.fold_in(keys[6], 2), own, number, TOK_DEV, EXPERTS, TOP, CAP, 2))(expert_ids_keys, expert_ids_turns).reshape((TOKENS, TOP))
    gate_counts = touch_ends(jax.random.randint(keys[7], (TOKENS, TOP), 1, 9), jax.random.fold_in(keys[7], 1), 1, 8).astype(jnp.int32)
    grad_out = gaussian(keys[8], (TOKENS, D), 1.0, 6.0, ((0, 128),))
    return dict(context=context, out_proj=out_proj, residual_in=residual_in, gain=gain, up_weight=up_weight, down_weight=down_weight, expert_ids=expert_ids, gate_counts=gate_counts, grad_out=grad_out)


def silu_slope(pre_act):
    sigmoid_value = jax.nn.sigmoid(pre_act)
    return sigmoid_value * (1.0 + pre_act * (1.0 - sigmoid_value))

def reference(context, out_proj, residual_in, gain, up_weight, down_weight, expert_ids, gate_counts, grad_out):
    tensor_groups = N_TENSOR
    head_cols = HEADS * HD // tensor_groups
    attention = jnp.zeros((TOKENS, D), jnp.float32)
    for group_index in range(tensor_groups):
        part_ctx = context[:, group_index * head_cols:(group_index + 1) * head_cols]
        part_proj = out_proj[group_index * head_cols:(group_index + 1) * head_cols]
        partial_value = jnp.dot(part_ctx, part_proj, preferred_element_type=jnp.float32).astype(jnp.bfloat16)
        partial_value = lax.optimization_barrier(partial_value)
        attention = attention + partial_value.astype(jnp.float32)
    hidden_in = residual_in.astype(jnp.float32) + attention
    inv_rms = lax.rsqrt(lax.optimization_barrier(jnp.mean(hidden_in * hidden_in, axis=1, keepdims=True)) + 1e-05)
    gain_f = gain.astype(jnp.float32)
    normed = (hidden_in * inv_rms * gain_f).astype(jnp.bfloat16)
    counts = gate_counts.astype(jnp.float32)
    weights = counts / lax.optimization_barrier(jnp.sum(counts, axis=1, keepdims=True))
    sources = N_EXPERT * N_TENSOR
    per_device = TOK_DEV * TOP
    routed_ids = expert_ids.reshape(sources, per_device)
    onehot = (routed_ids[:, :, None] == jnp.arange(EXPERTS, dtype=jnp.int32)[None, None, :]).astype(jnp.int32)
    earlier = jnp.cumsum(onehot, axis=1) - onehot
    slot_rank = lax.optimization_barrier(jnp.sum(earlier * onehot, axis=2))
    source_ids = jnp.arange(sources, dtype=jnp.int32)[:, None]
    positions = (routed_ids * (sources * CAP) + source_ids * CAP + slot_rank).reshape(-1).astype(jnp.int32)
    rows_all = EXPERTS * sources * CAP
    route_ids = jnp.arange(TOKENS * TOP, dtype=jnp.int32)
    route_table = jnp.zeros((rows_all,), jnp.int32).at[positions].set(route_ids).reshape(EXPERTS, sources * CAP)
    living = jnp.zeros((rows_all,), jnp.int32).at[positions].set(1).reshape(EXPERTS, sources * CAP)
    flat_weights = weights.reshape(-1)
    grad_f = grad_out.astype(jnp.float32)

    def expert_work(expert_item):
        up_rows, down_rows, routes, alive_flags = expert_item
        token_ids = routes // TOP
        row_mask = (alive_flags > 0)[:, None]
        inputs = jnp.where(row_mask, normed[token_ids], jnp.zeros((), jnp.bfloat16))
        scaled = (flat_weights[routes][:, None] * grad_f[token_ids]).astype(jnp.bfloat16)
        scaled = jnp.where(row_mask, scaled, jnp.zeros((), jnp.bfloat16))
        pre_act = jnp.dot(inputs, up_rows, preferred_element_type=jnp.float32)
        activated = jax.nn.silu(pre_act).astype(jnp.bfloat16)
        expert_out = jnp.dot(activated, down_rows, preferred_element_type=jnp.float32).astype(jnp.bfloat16)
        back_hidden = jnp.dot(scaled, down_rows.T, preferred_element_type=jnp.float32)
        grad_pre = (back_hidden * silu_slope(pre_act)).astype(jnp.bfloat16)
        grad_route = jnp.dot(grad_pre, up_rows.T, preferred_element_type=jnp.float32).astype(jnp.bfloat16)
        return (expert_out, grad_route)
    expert_outs, expert_grads = lax.map(expert_work, (up_weight, down_weight, route_table, living))
    out_routes = expert_outs.reshape(rows_all, D)[positions].reshape(TOKENS, TOP, D).astype(jnp.float32)
    expert_mix = lax.optimization_barrier(jnp.sum(weights[:, :, None] * out_routes, axis=1))
    mixed = (hidden_in + expert_mix).astype(jnp.bfloat16)
    grad_routes = expert_grads.reshape(rows_all, D)[positions].reshape(TOKENS, TOP, D).astype(jnp.float32)
    grad_normed = lax.optimization_barrier(jnp.sum(grad_routes, axis=1))
    scaled_grad = grad_normed * gain_f
    grad_hidden = grad_f + inv_rms * scaled_grad - hidden_in * inv_rms ** 3 * lax.optimization_barrier(jnp.mean(hidden_in * scaled_grad, axis=1, keepdims=True))
    grad_residual = grad_hidden.astype(jnp.bfloat16)
    grad_context = jnp.dot(grad_residual, out_proj.T, preferred_element_type=jnp.float32).astype(jnp.bfloat16)
    return (mixed, grad_residual, grad_context)
```

```python
import functools
import math

import jax
import jax.numpy as jnp
from jax import lax
from jax.experimental import pallas as pl
from jax.experimental.pallas import tpu as pltpu
from jax.sharding import PartitionSpec as P

CAP = 5
MESH = pl.DeviceIdType.MESH
F32, BF16 = jnp.float32, jnp.bfloat16
VMEM_LIMIT = 60 * 2**20


def chunks_of(width):
    step = -(-width // 3 // 128) * 128
    step = step + 128 if 3 * step < width else step
    return [(at, min(step, width - at)) for at in range(0, width, step)]


def tiles_of(width, step=512):
    return [(at, min(step, width - at)) for at in range(0, width, step)]


PLANE = [
    (0, 1), (1, 0), (0, 3), (3, 0), (1, 1), (3, 3), (1, 3), (3, 1),
    (0, 2), (2, 0), (1, 2), (2, 1), (3, 2), (2, 3), (2, 2),
]


class Place:
    def __init__(self):
        self.e, self.t = lax.axis_index("expert"), lax.axis_index("tensor")
        self.x, self.c = self.t // 2, lax.rem(self.t, 2)
        self.z, self.y = self.e // 4, lax.rem(self.e, 4)

    def column(self, step, other=False):
        core = 1 - self.c if other else self.c
        return lax.rem(self.x + step + 4, 4) * 2 + core

    def plane(self, offset):
        return lax.rem(self.z + offset[0], 4) * 4 + lax.rem(self.y + offset[1], 4)


class Wire:
    def __init__(self, send_sems, recv_sems):
        self.send_sems, self.recv_sems, self.count, self.sent = send_sems, recv_sems, 0, []

    def reserve(self):
        self.count += 1
        return self.count - 1

    def start(self, slot, src, dst, dev):
        copy = pltpu.make_async_remote_copy(
            src, dst, self.send_sems.at[slot], self.recv_sems.at[slot],
            device_id=dev, device_id_type=MESH,
        )
        copy.start()
        self.sent.append(copy)
        return copy

    def arrived(self, slot, landing):
        pltpu.make_async_copy(landing, landing, self.recv_sems.at[slot]).wait()

    def drain(self):
        for copy in self.sent:
            copy.wait_send()
        self.sent = []


class Gather:
    def __init__(self, place, wire, table):
        self.p, self.w, self.table = place, wire, table
        self.slots = [wire.reserve() for _ in range(8)]
        rows = table.shape[1]
        self.low, self.high = pl.ds(0, rows // 2), pl.ds(rows // 2, rows // 2)

    def begin(self):
        p, w, s, tab = self.p, self.w, self.slots, self.table
        own = tab.at[p.t]
        w.start(s[0], own, own, (p.e, p.column(1)))
        w.start(s[1], own, own, (p.e, p.column(-1)))
        w.start(s[2], own, own, (p.e, p.column(0, True)))

    def forward(self):
        p, w, s, tab = self.p, self.w, self.slots, self.table
        left, right = tab.at[p.column(-1)], tab.at[p.column(1)]
        partner = (p.e, p.column(0, True))
        w.arrived(s[0], left)
        near = tab.at[p.column(-1), self.low]
        w.start(s[3], near, near, (p.e, p.column(1)))
        w.start(s[5], left, left, partner)
        w.arrived(s[1], right)
        near = tab.at[p.column(1), self.high]
        w.start(s[4], near, near, (p.e, p.column(-1)))
        w.start(s[6], right, right, partner)

    def finish(self):
        p, w, s, tab = self.p, self.w, self.slots, self.table
        far = tab.at[p.column(2)]
        w.arrived(s[3], tab.at[p.column(2), self.low])
        w.arrived(s[4], tab.at[p.column(2), self.high])
        w.start(s[7], far, far, (p.e, p.column(0, True)))

    def settle(self):
        p, w, s, tab = self.p, self.w, self.slots, self.table
        for slot, step in ((s[2], 0), (s[5], -1), (s[6], 1), (s[7], 2)):
            w.arrived(slot, tab.at[p.column(step, True)])


class Scatter:
    def __init__(self, place, wire, part, cross, half, full):
        self.p, self.w = place, wire
        self.part, self.cross, self.half, self.full = part, cross, half, full
        self.slots = [wire.reserve() for _ in range(5)]
        rows = part.shape[2]
        self.low, self.high = pl.ds(0, rows // 2), pl.ds(rows // 2, rows // 2)

    def begin(self):
        p = self.p
        self.w.start(
            self.slots[0], self.part.at[1 - p.c], self.cross, (p.e, p.column(0, True))
        )

    def cores(self):
        p, w, s = self.p, self.w, self.slots
        w.arrived(s[0], self.cross)
        far = lax.rem(p.x + 2, 4)

        def add(at):
            mine = self.part[p.c, at].astype(F32)
            self.part[p.c, at] = (mine + self.cross[at].astype(F32)).astype(BF16)

        add(far)
        w.start(s[1], self.part.at[p.c, far, self.low], self.half.at[0], (p.e, p.column(1)))
        w.start(s[2], self.part.at[p.c, far, self.high], self.half.at[1], (p.e, p.column(-1)))
        add(lax.rem(p.x + 1, 4))
        add(lax.rem(p.x + 3, 4))
        add(p.x)

    def around(self):
        p, w, s = self.p, self.w, self.slots
        right, left = lax.rem(p.x + 1, 4), lax.rem(p.x + 3, 4)
        for slot, at, rows, side, step in (
            (0, right, self.low, 0, 1),
            (1, left, self.high, 1, -1),
        ):
            w.arrived(s[1 + slot], self.half.at[side])
            mine = self.part[p.c, at, rows].astype(F32)
            self.part[p.c, at, rows] = (mine + self.half[side].astype(F32)).astype(BF16)
            w.start(s[3 + slot], self.part.at[p.c, at], self.full.at[side], (p.e, p.column(step)))

    def result(self):
        p, w, s = self.p, self.w, self.slots
        w.arrived(s[3], self.full.at[0])
        w.arrived(s[4], self.full.at[1])
        total = self.part[p.c, p.x].astype(F32)
        return total + self.full[0].astype(F32) + self.full[1].astype(F32)


class Exchange:
    def __init__(self, place, src, dst, send_sem, recv_sem, own_sem):
        self.p, self.src, self.dst = place, src, dst
        self.sems = (send_sem, recv_sem, own_sem)

    def begin(self):
        p = self.p
        send_sem, recv_sem, own_sem = self.sems
        for offset in PLANE:
            peer = p.plane(offset)
            pltpu.make_async_remote_copy(
                self.src.at[peer], self.dst.at[p.e], send_sem, recv_sem,
                device_id=(peer, p.t), device_id_type=MESH,
            ).start()
        pltpu.make_async_copy(self.src.at[p.e], self.dst.at[p.e], own_sem).start()

    def arrived(self):
        p = self.p
        others = self.dst.at[pl.ds(0, len(PLANE))]
        pltpu.make_async_copy(others, others, self.sems[1]).wait()
        pltpu.make_async_copy(self.src.at[p.e], self.dst.at[p.e], self.sems[2]).wait()

    def drain(self):
        others = self.src.at[pl.ds(0, len(PLANE))]
        pltpu.make_async_copy(others, others, self.sems[0]).wait()


def greet(place):
    barrier = pltpu.get_barrier_semaphore()
    count = 0
    for core in (False, True):
        for step in range(4):
            if step or core:
                dev = (place.e, place.column(step, core))
                pl.semaphore_signal(barrier, inc=1, device_id=dev, device_id_type=MESH)
                count += 1
    for offset in PLANE:
        dev = (place.plane(offset), place.t)
        pl.semaphore_signal(barrier, inc=1, device_id=dev, device_id_type=MESH)
        count += 1
    pl.semaphore_wait(barrier, count)


def front_kernel(
    dims, context, out_proj, residual, gain, ids, counts, grad_out, *refs
):
    tok, width, group, slots = dims
    cuts = chunks_of(width)
    n = len(cuts)
    refs = list(refs)

    def take(k):
        out = refs[:k]
        del refs[:k]
        return out

    got_n, got_g = take(n), take(n)
    hidden, info = take(2)
    ctx, = take(1)
    proj = take(n)
    tab_n, tab_g = take(n), take(n)
    part, cross, half, full = take(n), take(n), take(n), take(n)
    out_n, out_g = take(n), take(n)
    pick, scale = take(2)
    send_sems, recv_sems, load_sems, plane_sems = refs

    p = Place()
    loads = [pltpu.make_async_copy(context, ctx, load_sems.at[0])]
    for j, (at, w) in enumerate(cuts):
        cols = pl.ds(at, w)
        loads.append(pltpu.make_async_copy(grad_out.at[:, cols], tab_g[j].at[p.t], load_sems.at[1 + j]))
    for j, (at, w) in enumerate(cuts):
        cols = pl.ds(at, w)
        loads.append(pltpu.make_async_copy(out_proj.at[:, cols], proj[j], load_sems.at[1 + n + j]))
    for load in loads:
        load.start()

    wire = Wire(send_sems, recv_sems)
    gather_g = [Gather(p, wire, tab_g[j]) for j in range(n)]
    gather_n = [Gather(p, wire, tab_n[j]) for j in range(n)]
    scatter = [Scatter(p, wire, part[j], cross[j], half[j], full[j]) for j in range(n)]
    swap_g = [Exchange(p, out_g[j], got_g[j], *(plane_sems.at[j, i] for i in range(3))) for j in range(n)]
    swap_n = [Exchange(p, out_n[j], got_n[j], *(plane_sems.at[n + j, i] for i in range(3))) for j in range(n)]
    info_slots = [wire.reserve() for _ in range(7)]

    experts = 128
    which = lax.broadcasted_iota(jnp.int32, (experts, tok), 0)
    route = [ids[k : k + 1, :] for k in range(4)]
    named = sum((which == r).astype(F32) for r in route)
    before = (
        lax.broadcasted_iota(jnp.int32, (tok, tok), 0)
        < lax.broadcasted_iota(jnp.int32, (tok, tok), 1)
    ).astype(BF16)
    earlier = jnp.dot(named.astype(BF16), before, preferred_element_type=F32)
    codes = []
    for r in route:
        rank = jnp.sum(jnp.where(which == r, earlier, 0.0), axis=0, keepdims=True)
        place = jnp.bitwise_and(r, 7) * slots + jnp.right_shift(r, 3) * group + p.t * CAP
        codes.append(place.astype(F32) + rank)
    info[p.t] = jnp.concatenate(codes + [counts[...].astype(F32)], axis=0)

    greet(p)
    for j in range(n):
        loads[1 + j].wait()
        gather_g[j].begin()
    where = [(s, c) for c in (False, True) for s in range(4) if s or c]
    for slot, (step, core) in zip(info_slots, where):
        wire.start(slot, info.at[p.t], info.at[p.t], (p.e, p.column(step, core)))
    loads[0].wait()

    def project(j):
        loads[1 + n + j].wait()
        w = cuts[j][1]

        @pl.loop(0, 4)
        def _(quarter):
            rows = pl.ds(pl.multiple_of(quarter * 2 * tok, 2 * tok), 2 * tok)
            lhs = ctx[rows, :]
            for at, size in tiles_of(w):
                got = jnp.dot(lhs, proj[j][:, at : at + size], preferred_element_type=F32)
                got = got.astype(BF16)
                part[j][0, quarter, :, at : at + size] = got[:tok]
                part[j][1, quarter, :, at : at + size] = got[tok:]

    for j in range(n):
        project(j)
        scatter[j].begin()
        gather_g[j].forward()

    for j in range(n):
        scatter[j].cores()

    for slot, (step, core) in zip(info_slots, where):
        wire.arrived(slot, info.at[p.column(-step, core)])

    @pl.loop(0, slots // 80)
    def _(block):
        first = block * 80 + p.t * slots
        slot_id = (lax.broadcasted_iota(jnp.int32, (80, tok), 0) + first).astype(F32)
        rows = pl.ds(pl.multiple_of(block * 80, 80), 80)
        weight = jnp.zeros((80, tok), F32)
        for s in range(8):
            facts = info[s]
            total = facts[4:5] + facts[5:6] + facts[6:7] + facts[7:8]
            hits = jnp.zeros((80, tok), F32)
            for k in range(4):
                hit = slot_id == facts[k : k + 1]
                hits = jnp.where(hit, 1.0, hits)
                weight = jnp.where(hit, facts[4 + k : 5 + k] / total, weight)
            pick[rows, s * tok : (s + 1) * tok] = hits.astype(BF16)
        scale[rows, :] = jnp.sum(weight, axis=1, keepdims=True)

    def select(j, table, out, weighted):
        w = cuts[j][1]
        part_rows = 8 * group

        @pl.loop(0, slots // part_rows)
        def _(block):
            rows = pl.ds(pl.multiple_of(block * part_rows, part_rows), part_rows)
            lhs = pick[rows, :]
            for at, size in tiles_of(w):
                rhs = table[:, :, at : at + size].reshape(8 * tok, size)
                got = jnp.dot(lhs, rhs, preferred_element_type=F32)
                if weighted:
                    got = got * scale[rows, :]
                out[pl.ds(block * 8, 8), :, at : at + size] = got.reshape(8, group, size).astype(BF16)

    gather_g[0].finish()
    gather_g[0].settle()
    select(0, tab_g[0], out_g[0], True)
    swap_g[0].begin()
    for j in range(n):
        scatter[j].around()
    for j in range(1, n):
        gather_g[j].finish()
    for j in range(1, n):
        gather_g[j].settle()
        select(j, tab_g[j], out_g[j], True)
        swap_g[j].begin()

    square = jnp.zeros((tok, 1), F32)
    for j, (at, w) in enumerate(cuts):
        value = residual[:, at : at + w].astype(F32) + scatter[j].result()
        hidden[:, at : at + w] = value
        square += jnp.sum(value * value, axis=1, keepdims=True)
    inv = lax.rsqrt(square / width + 1e-05)
    for j, (at, w) in enumerate(cuts):
        value = hidden[:, at : at + w] * inv * gain[:, at : at + w].astype(F32)
        tab_n[j][p.t] = value.astype(BF16)
        gather_n[j].begin()
    for j in range(n):
        gather_n[j].forward()
    for j in range(n):
        gather_n[j].finish()
        gather_n[j].settle()
        select(j, tab_n[j], out_n[j], False)
        swap_n[j].begin()
    for swap in swap_g + swap_n:
        swap.arrived()
        swap.drain()
    wire.drain()


def front(context, out_proj, residual, gain, ids, counts, grad_out, n_expert, n_tensor):
    tok, width = residual.shape
    rows, depth = context.shape
    group = n_tensor * CAP
    slots = n_expert * group
    cuts = chunks_of(width)
    n = len(cuts)
    hbm = pl.BlockSpec(memory_space=pl.ANY)
    vmem = pl.BlockSpec(memory_space=pltpu.VMEM)
    landing = [jax.ShapeDtypeStruct((n_expert, group, w), BF16) for _, w in cuts]
    per = lambda *lead: [pltpu.VMEM(lead + (w,), BF16) for _, w in cuts]
    copies = 16 * n + 5 * n + 7
    outs = pl.pallas_call(
        functools.partial(front_kernel, (tok, width, group, slots)),
        out_shape=tuple(
            landing * 2
            + [jax.ShapeDtypeStruct((tok, width), F32), jax.ShapeDtypeStruct((n_tensor, 8, tok), F32)]
        ),
        in_specs=[hbm, hbm, vmem, vmem, vmem, vmem, hbm],
        out_specs=tuple([hbm] * (2 * n) + [vmem] * 2),
        scratch_shapes=[pltpu.VMEM((rows, depth), BF16)]
        + per(depth)
        + per(n_tensor, tok) * 2
        + per(2, 4, tok)
        + per(4, tok)
        + per(2, tok // 2)
        + per(2, tok)
        + per(n_expert, group) * 2
        + [
            pltpu.VMEM((slots, n_tensor * tok), BF16),
            pltpu.VMEM((slots, 1), F32),
            pltpu.SemaphoreType.DMA((copies,)),
            pltpu.SemaphoreType.DMA((copies,)),
            pltpu.SemaphoreType.DMA((1 + 2 * n,)),
            pltpu.SemaphoreType.DMA((2 * n, 3)),
        ],
        compiler_params=pltpu.CompilerParams(
            collective_id=1, has_side_effects=True, vmem_limit_bytes=VMEM_LIMIT
        ),
        name="front",
    )(context, out_proj, residual, gain.reshape(1, width), ids, counts, grad_out)
    return outs[:n], outs[n : 2 * n], outs[2 * n], outs[2 * n + 1]


def silu_slope(pre_act):
    sigmoid_value = jax.nn.sigmoid(pre_act)
    return sigmoid_value * (1.0 + pre_act * (1.0 - sigmoid_value))


def local(
    context, out_proj, residual_in, gain, up_weight, down_weight, expert_ids, gate_counts, grad_out
):
    tok_rows, width = residual_in.shape
    n_expert = lax.axis_size("expert")
    n_tensor = lax.axis_size("tensor")
    t_me = lax.axis_index("tensor")
    group = n_tensor * CAP
    slots = n_expert * group
    got_n, got_g, hidden_in, info = front(
        context, out_proj, residual_in, gain, expert_ids.T, gate_counts.T, grad_out, n_expert, n_tensor
    )
    f32, bf16 = F32, BF16
    inputs = jnp.concatenate([a.reshape(slots, -1) for a in got_n], axis=1)
    cotangents = jnp.concatenate([a.reshape(slots, -1) for a in got_g], axis=1)
    inv_rms = lax.rsqrt(jnp.mean(hidden_in * hidden_in, axis=1, keepdims=True) + 1e-05)
    gain_f = gain.astype(f32)
    facts = info.transpose(0, 2, 1).reshape(n_tensor * tok_rows, 8)
    slot_all = facts[:, :4].astype(jnp.int32) - t_me * slots
    counts_all = facts[:, 4:]
    total_all = jnp.sum(counts_all, axis=1, keepdims=True)
    hit = slot_all[:, :, None] == jnp.arange(slots, dtype=jnp.int32)
    pick = jnp.any(hit, axis=1).astype(bf16)
    mix = jnp.sum(jnp.where(hit, counts_all[:, :, None], 0.0), axis=1).astype(bf16)

    def exchange(rows):
        return lax.all_to_all(rows, "expert", split_axis=0, concat_axis=0, tiled=True)

    up_rows = up_weight[0]
    down_rows = down_weight[0]
    pre_act = jnp.dot(inputs, up_rows, preferred_element_type=f32)
    activated = jax.nn.silu(pre_act).astype(bf16)
    expert_out = jnp.dot(activated, down_rows, preferred_element_type=f32).astype(bf16)
    back_out = exchange(expert_out)
    back_hidden = jnp.einsum("rd,fd->rf", cotangents, down_rows, preferred_element_type=f32)
    grad_pre = (back_hidden * silu_slope(pre_act)).astype(bf16)
    grad_route = jnp.einsum("rf,df->rd", grad_pre, up_rows, preferred_element_type=f32).astype(bf16)
    back_grad = exchange(grad_route)

    mix_part = (jnp.dot(mix, back_out, preferred_element_type=f32) / total_all).astype(bf16)
    expert_mix = lax.psum_scatter(mix_part, "tensor", scatter_dimension=0, tiled=True).astype(f32)
    mixed = (hidden_in + expert_mix).astype(bf16)
    grad_part = jnp.dot(pick, back_grad, preferred_element_type=f32).astype(bf16)
    grad_normed = lax.psum_scatter(grad_part, "tensor", scatter_dimension=0, tiled=True).astype(f32)
    scaled_grad = grad_normed * gain_f
    grad_hidden = (
        grad_out.astype(f32)
        + inv_rms * scaled_grad
        - hidden_in * inv_rms**3 * jnp.mean(hidden_in * scaled_grad, axis=1, keepdims=True)
    )
    grad_residual = grad_hidden.astype(bf16)
    grad_context = jnp.einsum(
        "td,cd->tc",
        lax.all_gather(grad_residual, "tensor", axis=0, tiled=True),
        out_proj,
        preferred_element_type=f32,
    ).astype(bf16)
    return (mixed, grad_residual, grad_context)


def solution(mesh):
    whole = P(("expert", "tensor"), None)
    in_specs = (
        P("expert", "tensor"),
        P("tensor", None),
        whole,
        P(),
        P(("expert", "tensor"), None, None),
        P(("expert", "tensor"), None, None),
        whole,
        whole,
        whole,
    )
    out_specs = (whole, whole, P("expert", "tensor"))
    return jax.shard_map(local, mesh=mesh, in_specs=in_specs, out_specs=out_specs, check_vma=False)
```

```python
import functools
import math

import jax
import jax.numpy as jnp
from jax import lax
from jax.experimental import pallas as pl
from jax.experimental.pallas import tpu as pltpu
from jax.sharding import PartitionSpec as P

CAP = 5
MESH = pl.DeviceIdType.MESH
F32, BF16 = jnp.float32, jnp.bfloat16
VMEM_LIMIT = 60 * 2**20


def chunks_of(width):
    step = -(-width // 3 // 128) * 128
    step = step + 128 if 3 * step < width else step
    return [(at, min(step, width - at)) for at in range(0, width, step)]


def dot_nt(a, b):
    return lax.dot_general(a, b, (((1,), (1,)), ((), ())), preferred_element_type=F32)


def tiles_of(width, step=512):
    return [(at, min(step, width - at)) for at in range(0, width, step)]


PLANE = [
    (0, 1), (1, 0), (0, 3), (3, 0), (1, 1), (3, 3), (1, 3), (3, 1),
    (0, 2), (2, 0), (1, 2), (2, 1), (3, 2), (2, 3), (2, 2),
]


class Place:
    def __init__(self):
        self.e, self.t = lax.axis_index("expert"), lax.axis_index("tensor")
        self.x, self.c = self.t // 2, lax.rem(self.t, 2)
        self.z, self.y = self.e // 4, lax.rem(self.e, 4)

    def column(self, step, other=False):
        core = 1 - self.c if other else self.c
        return lax.rem(self.x + step + 4, 4) * 2 + core

    def plane(self, offset):
        return lax.rem(self.z + offset[0], 4) * 4 + lax.rem(self.y + offset[1], 4)


class Wire:
    def __init__(self, send_sems, recv_sems):
        self.send_sems, self.recv_sems, self.count, self.sent = send_sems, recv_sems, 0, []

    def reserve(self):
        self.count += 1
        return self.count - 1

    def start(self, slot, src, dst, dev):
        copy = pltpu.make_async_remote_copy(
            src, dst, self.send_sems.at[slot], self.recv_sems.at[slot],
            device_id=dev, device_id_type=MESH,
        )
        copy.start()
        self.sent.append((slot, copy))

    def arrived(self, slot, landing):
        pltpu.make_async_copy(landing, landing, self.recv_sems.at[slot]).wait()

    def drain(self, slots=None):
        for slot, copy in self.sent:
            if slots is None or slot in slots:
                copy.wait_send()
        self.sent = [] if slots is None else [item for item in self.sent if item[0] not in slots]


class Gather:
    def __init__(self, place, wire, table, rows):
        self.p, self.w, self.table, self.rows = place, wire, table, rows
        self.slots = [wire.reserve() for _ in range(8)]

    def block(self, index, half=None):
        size = self.rows if half is None else self.rows // 2
        first = index * self.rows + (half or 0) * size
        return self.table.at[pl.ds(pl.multiple_of(first, size), size)]

    def begin(self):
        p, w, s = self.p, self.w, self.slots
        own = self.block(p.t)
        w.start(s[0], own, own, (p.e, p.column(1)))
        w.start(s[1], own, own, (p.e, p.column(-1)))
        w.start(s[2], own, own, (p.e, p.column(0, True)))

    def forward(self):
        p, w, s = self.p, self.w, self.slots
        left, right = self.block(p.column(-1)), self.block(p.column(1))
        partner = (p.e, p.column(0, True))
        w.arrived(s[0], left)
        near = self.block(p.column(-1), 0)
        w.start(s[3], near, near, (p.e, p.column(1)))
        w.start(s[5], left, left, partner)
        w.arrived(s[1], right)
        near = self.block(p.column(1), 1)
        w.start(s[4], near, near, (p.e, p.column(-1)))
        w.start(s[6], right, right, partner)

    def finish(self):
        p, w, s = self.p, self.w, self.slots
        far = self.block(p.column(2))
        w.arrived(s[3], self.block(p.column(2), 0))
        w.arrived(s[4], self.block(p.column(2), 1))
        w.start(s[7], far, far, (p.e, p.column(0, True)))

    def settle(self):
        p, w, s = self.p, self.w, self.slots
        for slot, step in ((s[2], 0), (s[5], -1), (s[6], 1), (s[7], 2)):
            w.arrived(slot, self.block(p.column(step, True)))


class Scatter:
    def __init__(self, place, wire, part, cross, half, full):
        self.p, self.w = place, wire
        self.part, self.cross, self.half, self.full = part, cross, half, full
        self.slots = [wire.reserve() for _ in range(5)]
        rows = part.shape[2]
        self.low, self.high = pl.ds(0, rows // 2), pl.ds(rows // 2, rows // 2)

    def begin(self):
        p = self.p
        self.w.start(
            self.slots[0], self.part.at[1 - p.c], self.cross, (p.e, p.column(0, True))
        )

    def cores(self):
        p, w, s = self.p, self.w, self.slots
        w.arrived(s[0], self.cross)
        far = lax.rem(p.x + 2, 4)

        def add(at):
            mine = self.part[p.c, at].astype(F32)
            self.part[p.c, at] = (mine + self.cross[at].astype(F32)).astype(BF16)

        add(far)
        w.start(s[1], self.part.at[p.c, far, self.low], self.half.at[0], (p.e, p.column(1)))
        w.start(s[2], self.part.at[p.c, far, self.high], self.half.at[1], (p.e, p.column(-1)))
        add(lax.rem(p.x + 1, 4))
        add(lax.rem(p.x + 3, 4))
        add(p.x)

    def around(self):
        p, w, s = self.p, self.w, self.slots
        right, left = lax.rem(p.x + 1, 4), lax.rem(p.x + 3, 4)
        for slot, at, rows, side, step in (
            (0, right, self.low, 0, 1),
            (1, left, self.high, 1, -1),
        ):
            w.arrived(s[1 + slot], self.half.at[side])
            mine = self.part[p.c, at, rows].astype(F32)
            self.part[p.c, at, rows] = (mine + self.half[side].astype(F32)).astype(BF16)
            w.start(s[3 + slot], self.part.at[p.c, at], self.full.at[side], (p.e, p.column(step)))

    def settle(self):
        self.w.arrived(self.slots[3], self.full.at[0])
        self.w.arrived(self.slots[4], self.full.at[1])

    def value(self):
        total = self.part[self.p.c, self.p.x].astype(F32)
        return total + self.full[0].astype(F32) + self.full[1].astype(F32)

    def release(self):
        self.w.drain(self.slots)


class Exchange:
    def __init__(self, place, src, dst, send_sem, recv_sem, own_sem):
        self.p, self.src, self.dst = place, src, dst
        self.sems = (send_sem, recv_sem, own_sem)

    def begin(self):
        p = self.p
        send_sem, recv_sem, own_sem = self.sems
        for offset in PLANE:
            peer = p.plane(offset)
            pltpu.make_async_remote_copy(
                self.src.at[peer], self.dst.at[p.e], send_sem, recv_sem,
                device_id=(peer, p.t), device_id_type=MESH,
            ).start()
        pltpu.make_async_copy(self.src.at[p.e], self.dst.at[p.e], own_sem).start()

    def arrived(self):
        p = self.p
        others = self.dst.at[pl.ds(0, len(PLANE))]
        pltpu.make_async_copy(others, others, self.sems[1]).wait()
        pltpu.make_async_copy(self.src.at[p.e], self.dst.at[p.e], self.sems[2]).wait()

    def drain(self):
        others = self.src.at[pl.ds(0, len(PLANE))]
        pltpu.make_async_copy(others, others, self.sems[0]).wait()


def greet(place):
    barrier = pltpu.get_barrier_semaphore()
    count = 0
    for core in (False, True):
        for step in range(4):
            if step or core:
                dev = (place.e, place.column(step, core))
                pl.semaphore_signal(barrier, inc=1, device_id=dev, device_id_type=MESH)
                count += 1
    for offset in PLANE:
        dev = (place.plane(offset), place.t)
        pl.semaphore_signal(barrier, inc=1, device_id=dev, device_id_type=MESH)
        count += 1
    pl.semaphore_wait(barrier, count)


def front_kernel(
    dims, context, out_proj, residual, gain, ids, counts, grad_out, *refs
):
    tok, width, group, slots = dims
    cuts = chunks_of(width)
    n = len(cuts)
    refs = list(refs)

    def take(k):
        out = refs[:k]
        del refs[:k]
        return out

    got_n, got_g = take(n), take(n)
    hidden, info = take(2)
    ctx, = take(1)
    proj = take(n)
    tab_n, tab_g = take(n), take(n)
    part, cross, half, full = take(n), take(n), take(n), take(n)
    out_n, out_g = take(n), take(n)
    pick, scale = take(2)
    send_sems, recv_sems, load_sems, plane_sems = refs

    p = Place()
    loads = [pltpu.make_async_copy(context, ctx, load_sems.at[0])]
    for j, (at, w) in enumerate(cuts):
        loads.append(pltpu.make_async_copy(out_proj.at[pl.ds(at, w)], proj[j], load_sems.at[1 + j]))
    for load in loads:
        load.start()

    wire = Wire(send_sems, recv_sems)
    own_rows = pl.ds(pl.multiple_of(p.t * tok, tok), tok)
    gather_g = [Gather(p, wire, tab_g[j], tok) for j in range(n)]
    gather_n = [Gather(p, wire, tab_n[j], tok) for j in range(n)]
    scatter = [Scatter(p, wire, part[j], cross[j], half[j], full[j]) for j in range(n)]
    swap_g = [Exchange(p, out_g[j], got_g[j], *(plane_sems.at[j, i] for i in range(3))) for j in range(n)]
    swap_n = [Exchange(p, out_n[j], got_n[j], *(plane_sems.at[n + j, i] for i in range(3))) for j in range(n)]
    info_slots = [wire.reserve() for _ in range(7)]

    experts = 128
    which = lax.broadcasted_iota(jnp.int32, (experts, tok), 0)
    route = [ids[k : k + 1, :] for k in range(4)]
    named = sum((which == r).astype(F32) for r in route)
    before = (
        lax.broadcasted_iota(jnp.int32, (tok, tok), 0)
        < lax.broadcasted_iota(jnp.int32, (tok, tok), 1)
    ).astype(BF16)
    earlier = jnp.dot(named.astype(BF16), before, preferred_element_type=F32)
    codes = []
    for r in route:
        rank = jnp.sum(jnp.where(which == r, earlier, 0.0), axis=0, keepdims=True)
        place = jnp.bitwise_and(r, 7) * slots + jnp.right_shift(r, 3) * group + p.t * CAP
        codes.append(place.astype(F32) + rank)
    info[p.t] = jnp.concatenate(codes + [counts[...].astype(F32)], axis=0)

    for j, (at, w) in enumerate(cuts):
        tab_g[j][own_rows, :] = grad_out[at : at + w, :].astype(F32).T.astype(BF16)
    greet(p)
    for j in range(n):
        gather_g[j].begin()
    where = [(s, c) for c in (False, True) for s in range(4) if s or c]
    for slot, (step, core) in zip(info_slots, where):
        wire.start(slot, info.at[p.t], info.at[p.t], (p.e, p.column(step, core)))
    loads[0].wait()

    def project(j):
        loads[1 + j].wait()
        w = cuts[j][1]

        @pl.loop(0, 4)
        def _(quarter):
            rows = pl.ds(pl.multiple_of(quarter * 2 * tok, 2 * tok), 2 * tok)
            lhs = ctx[rows, :]
            for at, size in tiles_of(w):
                got = dot_nt(lhs, proj[j][at : at + size, :]).astype(BF16)
                part[j][0, quarter, :, at : at + size] = got[:tok]
                part[j][1, quarter, :, at : at + size] = got[tok:]

    for j in range(n):
        project(j)
        scatter[j].begin()
        gather_g[j].forward()

    for j in range(n):
        scatter[j].cores()

    for slot, (step, core) in zip(info_slots, where):
        wire.arrived(slot, info.at[p.column(-step, core)])

    @pl.loop(0, slots // 80)
    def _(block):
        first = block * 80 + p.t * slots
        slot_id = (lax.broadcasted_iota(jnp.int32, (80, tok), 0) + first).astype(F32)
        rows = pl.ds(pl.multiple_of(block * 80, 80), 80)
        weight = jnp.zeros((80, tok), F32)
        for s in range(8):
            facts = info[s]
            total = facts[4:5] + facts[5:6] + facts[6:7] + facts[7:8]
            hits = jnp.zeros((80, tok), F32)
            for k in range(4):
                hit = slot_id == facts[k : k + 1]
                hits = jnp.where(hit, 1.0, hits)
                weight = jnp.where(hit, facts[4 + k : 5 + k] / total, weight)
            pick[rows, s * tok : (s + 1) * tok] = hits.astype(BF16)
        scale[rows, :] = jnp.sum(weight, axis=1, keepdims=True)

    def select(j, table, out, weighted):
        w = cuts[j][1]
        part_rows = 8 * group

        @pl.loop(0, slots // part_rows)
        def _(block):
            rows = pl.ds(pl.multiple_of(block * part_rows, part_rows), part_rows)
            lhs = pick[rows, :]
            for at, size in tiles_of(w):
                got = jnp.dot(lhs, table[:, at : at + size], preferred_element_type=F32)
                if weighted:
                    got = got * scale[rows, :]
                out[pl.ds(block * 8, 8), :, at : at + size] = got.reshape(8, group, size).astype(BF16)

    gather_g[0].finish()
    gather_g[0].settle()
    select(0, tab_g[0], out_g[0], True)
    swap_g[0].begin()
    for j in range(n):
        scatter[j].around()
    for j in range(1, n):
        gather_g[j].finish()
    for j in range(1, n):
        gather_g[j].settle()
        select(j, tab_g[j], out_g[j], True)
        swap_g[j].begin()

    square = jnp.zeros((tok, 1), F32)
    for j, (at, w) in enumerate(cuts):
        scatter[j].settle()
        value = residual[at : at + w, :].astype(F32).T + scatter[j].value()
        hidden[:, at : at + w] = value
        square += jnp.sum(value * value, axis=1, keepdims=True)
    inv = lax.rsqrt(square / width + 1e-05)
    for j, (at, w) in enumerate(cuts):
        value = hidden[:, at : at + w] * inv * gain[:, at : at + w].astype(F32)
        tab_n[j][own_rows, :] = value.astype(BF16)
        gather_n[j].begin()
    for j in range(n):
        gather_n[j].forward()
    for j in range(n):
        gather_n[j].finish()
        gather_n[j].settle()
        select(j, tab_n[j], out_n[j], False)
        swap_n[j].begin()
    for swap in swap_g + swap_n:
        swap.arrived()
        swap.drain()
    wire.drain()


def front(context, out_proj, residual, gain, ids, counts, grad_out, n_expert, n_tensor):
    width, tok = residual.shape
    rows, depth = context.shape
    group = n_tensor * CAP
    slots = n_expert * group
    cuts = chunks_of(width)
    n = len(cuts)
    hbm = pl.BlockSpec(memory_space=pl.ANY)
    vmem = pl.BlockSpec(memory_space=pltpu.VMEM)
    landing = [jax.ShapeDtypeStruct((n_expert, group, w), BF16) for _, w in cuts]
    per = lambda *lead: [pltpu.VMEM(lead + (w,), BF16) for _, w in cuts]
    copies = 16 * n + 5 * n + 7
    outs = pl.pallas_call(
        functools.partial(front_kernel, (tok, width, group, slots)),
        out_shape=tuple(
            landing * 2
            + [jax.ShapeDtypeStruct((tok, width), F32), jax.ShapeDtypeStruct((n_tensor, 8, tok), F32)]
        ),
        in_specs=[hbm, hbm, vmem, vmem, vmem, vmem, vmem],
        out_specs=tuple([hbm] * (2 * n) + [vmem] * 2),
        scratch_shapes=[pltpu.VMEM((rows, depth), BF16)]
        + [pltpu.VMEM((w, depth), BF16) for _, w in cuts]
        + per(n_tensor * tok) * 2
        + per(2, 4, tok)
        + per(4, tok)
        + per(2, tok // 2)
        + per(2, tok)
        + per(n_expert, group) * 2
        + [
            pltpu.VMEM((slots, n_tensor * tok), BF16),
            pltpu.VMEM((slots, 1), F32),
            pltpu.SemaphoreType.DMA((copies,)),
            pltpu.SemaphoreType.DMA((copies,)),
            pltpu.SemaphoreType.DMA((1 + n,)),
            pltpu.SemaphoreType.DMA((2 * n, 3)),
        ],
        compiler_params=pltpu.CompilerParams(
            collective_id=1, has_side_effects=True, vmem_limit_bytes=VMEM_LIMIT
        ),
        name="front",
    )(context, out_proj, residual, gain.reshape(1, width), ids, counts, grad_out)
    return outs[:n], outs[n : 2 * n], outs[2 * n], outs[2 * n + 1]


def back_kernel(dims, inner, *refs):
    tok, width, group, slots = dims
    cuts = chunks_of(width)
    n = len(cuts)
    refs = list(refs)

    def take(k):
        out = refs[:k]
        del refs[:k]
        return out

    got_n, got_g = take(n), take(n)
    up_t, down, proj_t, info, hidden, gain, grad_t = take(7)
    mixed, residual, grad_context = take(3)
    land_o, land_g = take(n), take(n)
    rows_n, rows_g, rows_o = take(n), take(n), take(n)
    up, low = take(n), take(n)
    proj, pre, act, pick, mix, total, acc = take(7)
    part = take(n)
    cross_o, half_o, full_o = take(n), take(n), take(n)
    cross_g, half_g, full_g = take(n), take(n), take(n)
    send_sems, recv_sems, load_sems, plane_sems, late_sems = refs

    p = Place()
    loads = []
    for j, (at, w) in enumerate(cuts):
        cols = pl.ds(at, w)
        loads.append(
            (
                pltpu.make_async_copy(got_n[j], rows_n[j], load_sems.at[j, 0]),
                pltpu.make_async_copy(up_t.at[:, cols], up[j], load_sems.at[j, 1]),
                pltpu.make_async_copy(down.at[:, cols], low[j], load_sems.at[j, 2]),
                pltpu.make_async_copy(got_g[j], rows_g[j], load_sems.at[j, 3]),
            )
        )
    for kind in range(4):
        for j in range(n):
            loads[j][kind].start()
    load_proj = pltpu.make_async_copy(proj_t, proj, load_sems.at[n, 0])
    load_proj.start()

    wire = Wire(send_sems, recv_sems)
    sum_o = [Scatter(p, wire, part[j], cross_o[j], half_o[j], full_o[j]) for j in range(n)]
    sum_g = [Scatter(p, wire, part[j], cross_g[j], half_g[j], full_g[j]) for j in range(n)]
    gather = [Gather(p, wire, up[j], tok) for j in range(n)]
    swap_o = [Exchange(p, rows_o[j], land_o[j], *(plane_sems.at[j, i] for i in range(3))) for j in range(n)]
    swap_g = [Exchange(p, rows_n[j], land_g[j], *(plane_sems.at[n + j, i] for i in range(3))) for j in range(n)]

    greet(p)
    tiles = inner // act.shape[2]
    depth = act.shape[2]
    span = 8 * group

    def tile_rows(i):
        return pl.ds(pl.multiple_of(i * depth, depth), depth)

    def block_rows(b):
        return pl.ds(pl.multiple_of(b * span, span), span)

    def peers(b):
        return pl.ds(b * 8, 8)

    for j in range(n):
        loads[j][0].wait()
        loads[j][1].wait()

    @pl.loop(0, tiles)
    def _(i):
        @pl.loop(0, slots // span)
        def _(b):
            value = sum(
                dot_nt(rows_n[j][peers(b)].reshape(span, cuts[j][1]), up[j][tile_rows(i), :])
                for j in range(n)
            )
            pre[i, block_rows(b), :] = value
            act[i, block_rows(b), :] = (value / (1.0 + jnp.exp(-value))).astype(BF16)

    def widen(weight, j, out):
        @pl.loop(0, slots // span)
        def _(b):
            for at, size in tiles_of(cuts[j][1]):
                value = sum(
                    jnp.dot(
                        act[i, block_rows(b), :],
                        weight[j][i * depth : (i + 1) * depth, at : at + size],
                        preferred_element_type=F32,
                    )
                    for i in range(tiles)
                )
                out[peers(b), :, at : at + size] = value.reshape(8, group, size).astype(BF16)

    for j in range(n):
        loads[j][2].wait()
        widen(low, j, rows_o[j])
        swap_o[j].begin()

    for j in range(n):
        loads[j][3].wait()

    @pl.loop(0, tiles)
    def _(i):
        @pl.loop(0, slots // span)
        def _(b):
            value = sum(
                dot_nt(rows_g[j][peers(b)].reshape(span, cuts[j][1]), low[j][tile_rows(i), :])
                for j in range(n)
            )
            before = pre[i, block_rows(b), :]
            gate = 1.0 / (1.0 + jnp.exp(-before))
            act[i, block_rows(b), :] = (value * (gate * (1.0 + before * (1.0 - gate)))).astype(BF16)

    for j in range(n):
        widen(up, j, rows_n[j])
        swap_g[j].begin()

    @pl.loop(0, 8)
    def _(s):
        facts = jnp.concatenate([info[s], jnp.zeros((tok - 8, tok), F32)], axis=0).T
        slot_id = (lax.broadcasted_iota(jnp.int32, (tok, slots), 1) + p.t * slots).astype(F32)
        hits = jnp.zeros((tok, slots), F32)
        taken = jnp.zeros((tok, slots), F32)
        for k in range(4):
            hit = slot_id == facts[:, k : k + 1]
            hits = jnp.where(hit, 1.0, hits)
            taken = jnp.where(hit, facts[:, 4 + k : 5 + k], taken)
        rows = pl.ds(pl.multiple_of(s * tok, tok), tok)
        pick[rows, :] = hits.astype(BF16)
        mix[rows, :] = taken.astype(BF16)
        total[rows, :] = facts[:, 4:5] + facts[:, 5:6] + facts[:, 6:7] + facts[:, 7:8]

    def combine(j, table, rows, shared):
        @pl.loop(0, 4)
        def _(quarter):
            span2 = pl.ds(pl.multiple_of(quarter * 2 * tok, 2 * tok), 2 * tok)
            lhs = table[span2, :]
            for at, size in tiles_of(cuts[j][1]):
                rhs = rows[:, :, at : at + size].reshape(slots, size)
                value = jnp.dot(lhs, rhs, preferred_element_type=F32)
                if shared:
                    value = value / total[span2, :]
                value = value.astype(BF16)
                part[j][0, quarter, :, at : at + size] = value[:tok]
                part[j][1, quarter, :, at : at + size] = value[tok:]

    def fetch(swap, j, kind, rows):
        swap.arrived()
        load = pltpu.make_async_copy(swap.dst, rows, late_sems.at[j, kind])
        load.start()
        load.wait()

    def mixed_out(j):
        at, w = cuts[j]
        sum_o[j].settle()
        mixed[:, at : at + w] = (hidden[:, at : at + w] + sum_o[j].value()).astype(BF16)
        sum_o[j].release()

    for j in range(n):
        fetch(swap_o[j], j, 0, rows_g[j])
        combine(j, mix, rows_g[j], True)
        sum_o[j].begin()
        if j >= 1:
            sum_o[j - 1].cores()
        if j >= 2:
            sum_o[j - 2].around()
    sum_o[n - 1].cores()
    for j in range(max(n - 2, 0), n):
        sum_o[j].around()
    for j in range(n):
        mixed_out(j)

    for j in range(n):
        swap_o[j].drain()
        fetch(swap_g[j], j, 1, rows_o[j])
        combine(j, pick, rows_o[j], False)
        sum_g[j].begin()
        if j >= 1:
            sum_g[j - 1].cores()
        if j >= 2:
            sum_g[j - 2].around()
    sum_g[n - 1].cores()
    for j in range(max(n - 2, 0), n):
        sum_g[j].around()

    square = jnp.zeros((tok, 1), F32)
    cross = jnp.zeros((tok, 1), F32)
    for j, (at, w) in enumerate(cuts):
        sum_g[j].settle()
        here = hidden[:, at : at + w]
        square += jnp.sum(here * here, axis=1, keepdims=True)
        scaled = sum_g[j].value() * gain[:, at : at + w].astype(F32)
        cross += jnp.sum(here * scaled, axis=1, keepdims=True)
    inv = lax.rsqrt(square / width + 1e-05)
    slope = inv * inv * inv * (cross / width)
    own_rows = pl.ds(pl.multiple_of(p.t * tok, tok), tok)
    for j, (at, w) in enumerate(cuts):
        scaled = sum_g[j].value() * gain[:, at : at + w].astype(F32)
        value = grad_t[at : at + w, :].astype(F32).T + inv * scaled - hidden[:, at : at + w] * slope
        value = value.astype(BF16)
        up[j][own_rows, :] = value
        gather[j].begin()
        residual[:, at : at + w] = value
    load_proj.wait()
    for j in range(n):
        gather[j].forward()
    for j, (at, w) in enumerate(cuts):
        gather[j].finish()
        gather[j].settle()

        @pl.loop(0, 4)
        def _(quarter):
            rows = pl.ds(pl.multiple_of(quarter * 2 * tok, 2 * tok), 2 * tok)
            value = jnp.dot(up[j][rows, :], proj[at : at + w, :], preferred_element_type=F32)
            if j > 0:
                value += acc[rows, :]
            if j < n - 1:
                acc[rows, :] = value
            else:
                grad_context[rows, :] = value.astype(BF16)

    for swap in swap_g:
        swap.drain()
    wire.drain()


def back(got_n, got_g, up_t, down, proj_t, info, hidden, gain, grad_t, n_expert, n_tensor):
    tok, width = hidden.shape
    inner = down.shape[0]
    depth = proj_t.shape[1]
    group = n_tensor * CAP
    slots = n_expert * group
    cuts = chunks_of(width)
    n = len(cuts)
    hbm = pl.BlockSpec(memory_space=pl.ANY)
    vmem = pl.BlockSpec(memory_space=pltpu.VMEM)
    landing = [jax.ShapeDtypeStruct((n_expert, group, w), BF16) for _, w in cuts]
    per = lambda *lead: [pltpu.VMEM(lead + (w,), BF16) for _, w in cuts]
    copies = (8 + 5 + 5) * n
    tiles = 3
    outs = pl.pallas_call(
        functools.partial(back_kernel, (tok, width, group, slots), inner),
        out_shape=(
            jax.ShapeDtypeStruct((tok, width), BF16),
            jax.ShapeDtypeStruct((tok, width), BF16),
            jax.ShapeDtypeStruct((n_tensor * tok, depth), BF16),
            *landing * 2,
        ),
        in_specs=[hbm] * (2 * n) + [hbm, hbm, hbm, vmem, vmem, vmem, vmem],
        out_specs=tuple([vmem] * 3 + [hbm] * (2 * n)),
        scratch_shapes=per(n_expert, group) * 3
        + per(inner) * 2
        + [
            pltpu.VMEM((width, depth), BF16),
            pltpu.VMEM((tiles, slots, inner // tiles), F32),
            pltpu.VMEM((tiles, slots, inner // tiles), BF16),
            pltpu.VMEM((n_tensor * tok, slots), BF16),
            pltpu.VMEM((n_tensor * tok, slots), BF16),
            pltpu.VMEM((n_tensor * tok, 1), F32),
            pltpu.VMEM((n_tensor * tok, depth), F32),
        ]
        + per(2, 4, tok)
        + (per(4, tok) + per(2, tok // 2) + per(2, tok)) * 2
        + [
            pltpu.SemaphoreType.DMA((copies,)),
            pltpu.SemaphoreType.DMA((copies,)),
            pltpu.SemaphoreType.DMA((n + 1, 4)),
            pltpu.SemaphoreType.DMA((2 * n, 3)),
            pltpu.SemaphoreType.DMA((n, 2)),
        ],
        compiler_params=pltpu.CompilerParams(
            collective_id=2, has_side_effects=True, vmem_limit_bytes=VMEM_LIMIT + 3 * 2**20
        ),
        name="back",
    )(*got_n, *got_g, up_t, down, proj_t, info, hidden, gain, grad_t)
    return outs[:3]


def local(
    context, out_proj, residual_in, gain, up_weight, down_weight, expert_ids, gate_counts, grad_out
):
    n_expert = lax.axis_size("expert")
    n_tensor = lax.axis_size("tensor")
    gain_row = gain.reshape(1, -1)
    got_n, got_g, hidden_in, info = front(
        context, out_proj.T, residual_in.T, gain_row, expert_ids.T, gate_counts.T, grad_out.T,
        n_expert, n_tensor,
    )
    return back(
        got_n, got_g, up_weight[0].T, down_weight[0], out_proj.T, info, hidden_in, gain_row,
        grad_out.T, n_expert, n_tensor,
    )


def solution(mesh):
    whole = P(("expert", "tensor"), None)
    in_specs = (
        P("expert", "tensor"),
        P("tensor", None),
        whole,
        P(),
        P(("expert", "tensor"), None, None),
        P(("expert", "tensor"), None, None),
        whole,
        whole,
        whole,
    )
    out_specs = (whole, whole, P("expert", "tensor"))
    return jax.shard_map(local, mesh=mesh, in_specs=in_specs, out_specs=out_specs, check_vma=False)
```

```python
import functools
import math

import jax
import jax.numpy as jnp
from jax import lax
from jax.experimental import pallas as pl
from jax.experimental.pallas import tpu as pltpu
from jax.sharding import PartitionSpec as P

CAP = 5
STARTS = (0, 640, 1408, 2176)
MESH = pl.DeviceIdType.MESH
F32, BF16 = jnp.float32, jnp.bfloat16
VMEM_LIMIT = 65000 * 2**10


def chunks_of(width):
    starts = STARTS + (width,)
    return [(at, end - at) for at, end in zip(starts, starts[1:])]


def dot_nt(a, b):
    return lax.dot_general(a, b, (((1,), (1,)), ((), ())), preferred_element_type=F32)


def tiles_of(width, step=512):
    return [(at, min(step, width - at)) for at in range(0, width, step)]


PLANE = [
    (0, 1), (1, 0), (0, 3), (3, 0), (1, 1), (3, 3), (1, 3), (3, 1),
    (0, 2), (2, 0), (1, 2), (2, 1), (3, 2), (2, 3), (2, 2),
]


class Place:
    def __init__(self):
        self.e, self.t = lax.axis_index("expert"), lax.axis_index("tensor")
        self.x, self.c = self.t // 2, lax.rem(self.t, 2)
        self.z, self.y = self.e // 4, lax.rem(self.e, 4)

    def column(self, step, other=False):
        core = 1 - self.c if other else self.c
        return lax.rem(self.x + step + 4, 4) * 2 + core

    def plane(self, offset):
        return lax.rem(self.z + offset[0], 4) * 4 + lax.rem(self.y + offset[1], 4)


class Wire:
    def __init__(self, send_sems, recv_sems):
        self.send_sems, self.recv_sems, self.count, self.sent = send_sems, recv_sems, 0, []

    def reserve(self):
        self.count += 1
        return self.count - 1

    def start(self, slot, src, dst, dev):
        copy = pltpu.make_async_remote_copy(
            src, dst, self.send_sems.at[slot], self.recv_sems.at[slot],
            device_id=dev, device_id_type=MESH,
        )
        copy.start()
        self.sent.append((slot, copy))

    def arrived(self, slot, landing):
        pltpu.make_async_copy(landing, landing, self.recv_sems.at[slot]).wait()

    def drain(self, slots=None):
        for slot, copy in self.sent:
            if slots is None or slot in slots:
                copy.wait_send()
        self.sent = [] if slots is None else [item for item in self.sent if item[0] not in slots]


class Gather:
    def __init__(self, place, wire, table, rows):
        self.p, self.w, self.table, self.rows = place, wire, table, rows
        self.slots = [wire.reserve() for _ in range(8)]

    def block(self, index, half=None):
        size = self.rows if half is None else self.rows // 2
        first = index * self.rows + (half or 0) * size
        return self.table.at[pl.ds(pl.multiple_of(first, size), size)]

    def begin(self):
        p, w, s = self.p, self.w, self.slots
        own = self.block(p.t)
        w.start(s[0], own, own, (p.e, p.column(1)))
        w.start(s[1], own, own, (p.e, p.column(-1)))
        w.start(s[2], own, own, (p.e, p.column(0, True)))

    def forward(self):
        p, w, s = self.p, self.w, self.slots
        left, right = self.block(p.column(-1)), self.block(p.column(1))
        partner = (p.e, p.column(0, True))
        w.arrived(s[0], left)
        near = self.block(p.column(-1), 0)
        w.start(s[3], near, near, (p.e, p.column(1)))
        w.start(s[5], left, left, partner)
        w.arrived(s[1], right)
        near = self.block(p.column(1), 1)
        w.start(s[4], near, near, (p.e, p.column(-1)))
        w.start(s[6], right, right, partner)

    def finish(self):
        p, w, s = self.p, self.w, self.slots
        far = self.block(p.column(2))
        w.arrived(s[3], self.block(p.column(2), 0))
        w.arrived(s[4], self.block(p.column(2), 1))
        w.start(s[7], far, far, (p.e, p.column(0, True)))

    def settle(self):
        p, w, s = self.p, self.w, self.slots
        for slot, step in ((s[2], 0), (s[5], -1), (s[6], 1), (s[7], 2)):
            w.arrived(slot, self.block(p.column(step, True)))


class Scatter:
    def __init__(self, place, wire, part, cross, half, full):
        self.p, self.w = place, wire
        self.part, self.cross, self.half, self.full = part, cross, half, full
        self.slots = [wire.reserve() for _ in range(5)]
        self.rows = full.shape[1]

    def at(self, core, x, half=None):
        size = self.rows if half is None else self.rows // 2
        first = (core * 4 + x) * self.rows + (half or 0) * size
        return pl.ds(pl.multiple_of(first, size), size)

    def begin(self):
        p = self.p
        theirs = pl.ds(pl.multiple_of((1 - p.c) * 4 * self.rows, 4 * self.rows), 4 * self.rows)
        self.w.start(self.slots[0], self.part.at[theirs], self.cross, (p.e, p.column(0, True)))

    def cores(self):
        p, w, s = self.p, self.w, self.slots
        w.arrived(s[0], self.cross)
        far = lax.rem(p.x + 2, 4)

        def add(x):
            rows = self.at(p.c, x)
            theirs = pl.ds(pl.multiple_of(x * self.rows, self.rows), self.rows)
            mine = self.part[rows, :].astype(F32)
            self.part[rows, :] = (mine + self.cross[theirs, :].astype(F32)).astype(BF16)

        add(far)
        w.start(s[1], self.part.at[self.at(p.c, far, 0)], self.half.at[0], (p.e, p.column(1)))
        w.start(s[2], self.part.at[self.at(p.c, far, 1)], self.half.at[1], (p.e, p.column(-1)))
        add(lax.rem(p.x + 1, 4))
        add(lax.rem(p.x + 3, 4))
        add(p.x)

    def around(self):
        p, w, s = self.p, self.w, self.slots
        for side, step in ((0, 1), (1, -1)):
            x = lax.rem(p.x + step + 4, 4)
            w.arrived(s[1 + side], self.half.at[side])
            rows = self.at(p.c, x, side)
            mine = self.part[rows, :].astype(F32)
            self.part[rows, :] = (mine + self.half[side].astype(F32)).astype(BF16)
            w.start(
                s[3 + side], self.part.at[self.at(p.c, x)], self.full.at[side],
                (p.e, p.column(step)),
            )

    def settle(self):
        self.w.arrived(self.slots[3], self.full.at[0])
        self.w.arrived(self.slots[4], self.full.at[1])

    def value(self):
        total = self.part[self.at(self.p.c, self.p.x), :].astype(F32)
        return total + self.full[0].astype(F32) + self.full[1].astype(F32)

    def release(self):
        self.w.drain(self.slots)


class Exchange:
    def __init__(self, place, src, dst, send_sem, recv_sem, own_sem):
        self.p, self.src, self.dst = place, src, dst
        self.sems = (send_sem, recv_sem, own_sem)

    def begin(self):
        p = self.p
        send_sem, recv_sem, own_sem = self.sems
        for offset in PLANE:
            peer = p.plane(offset)
            pltpu.make_async_remote_copy(
                self.src.at[peer], self.dst.at[p.e], send_sem, recv_sem,
                device_id=(peer, p.t), device_id_type=MESH,
            ).start()
        pltpu.make_async_copy(self.src.at[p.e], self.dst.at[p.e], own_sem).start()

    def arrived(self):
        p = self.p
        others = self.dst.at[pl.ds(0, len(PLANE))]
        pltpu.make_async_copy(others, others, self.sems[1]).wait()
        pltpu.make_async_copy(self.src.at[p.e], self.dst.at[p.e], self.sems[2]).wait()

    def drain(self):
        others = self.src.at[pl.ds(0, len(PLANE))]
        pltpu.make_async_copy(others, others, self.sems[0]).wait()


def greet(place):
    barrier = pltpu.get_barrier_semaphore()
    count = 0
    for core in (False, True):
        for step in range(4):
            if step or core:
                dev = (place.e, place.column(step, core))
                pl.semaphore_signal(barrier, inc=1, device_id=dev, device_id_type=MESH)
                count += 1
    for offset in PLANE:
        dev = (place.plane(offset), place.t)
        pl.semaphore_signal(barrier, inc=1, device_id=dev, device_id_type=MESH)
        count += 1
    pl.semaphore_wait(barrier, count)


ORDER = (
    "ggB0", "P0", "P1", "P2", "saC0", "ggF0", "ggB1", "ggB2", "P3", "saC1",
    "CH", "saA0", "saC2", "ggE0", "saC3", "ggF1", "SG0", "ggF2", "saA1", "G0",
    "H0", "saA2", "saA3", "ggE1", "ggE2", "SG1", "SG2", "H1", "G1", "gnF0",
    "G2", "H2", "H3", "R", "gnF1", "RS", "gnE0", "SN0", "gnF2", "ggB3",
    "N0", "gnF3", "gnE1", "gnE2", "SN1", "SN2", "ggF3", "gnE3", "N1", "ggE3",
    "SN3", "SG3", "PK", "N2", "G3", "N3", "PARK", "FWD", "CT0", "CT1",
    "CT2", "O0", "CT3", "O1", "O2", "O3", "BH", "LO0", "B0", "B1",
    "LO1", "B2", "B3", "CO0", "CO1", "soC0", "LO2", "soC1", "soA0", "CO2",
    "soA1", "soC2", "MX0", "LO3", "CO3", "soA2", "soC3", "MX1", "LB0", "CB0",
    "soA3", "MX2", "sgC0", "sgA0", "LB1", "MX3", "CB1", "Q0", "sgC1", "grF0",
    "sgA1", "LB2", "grE0", "CB2", "AC0", "Q1", "sgC2", "LB3", "grF1", "CB3",
    "sgA2", "grE1", "sgC3", "AC1", "Q2", "sgA3", "grF2", "Q3", "M", "grE2",
    "RES", "AC2", "grF3", "grE3", "AC3", "END",
)


class Column:
    def __init__(self, ref, index, size):
        self.ref, self.index, self.size = ref, index, size

    def rows(self, key):
        if key is Ellipsis:
            return pl.ds(0, self.size)
        return key[0]

    def __getitem__(self, key):
        return self.ref[self.rows(key), self.index : self.index + 1]

    def __setitem__(self, key, value):
        self.ref[self.rows(key), self.index : self.index + 1] = value


def kernel(dims, *refs):
    tok, width, group, slots, inner = dims
    cuts = chunks_of(width)
    n = len(cuts)
    refs = list(refs)

    def take(k):
        out = refs[:k]
        del refs[:k]
        return out

    context, proj_t, res_t, gain, ids, counts, grad_t, up_t, down = take(9)
    mixed_t, residual_t, grad_context, park = take(4)
    land_g, land_o, land_b = take(n), take(n), take(n)
    rows_a, rows_b, rows_c = take(n), take(n), take(n)
    up, low = take(n), take(n)
    proj, hidden, info, pre, act, maps, cols = take(7)
    roots, root_out, root_in, slopes = take(4)
    part = take(n)
    cross_a, half_a, full_a = take(n), take(n), take(n)
    cross_b, half_b, full_b = take(n), take(n), take(n)
    send_sems, recv_sems, load_sems, plane_sems = refs

    p = Place()
    ctx = grad_context
    wire = Wire(send_sems, recv_sems)
    gather_g = [Gather(p, wire, up[j], tok) for j in range(n)]
    gather_n = [Gather(p, wire, low[j], tok) for j in range(n)]
    gather_r = [Gather(p, wire, up[j], tok) for j in range(n)]
    sum_a = [Scatter(p, wire, part[j], cross_a[j], half_a[j], full_a[j]) for j in range(n)]
    sum_o = [Scatter(p, wire, low[j], cross_b[j], half_b[j], full_b[j]) for j in range(n)]
    sum_g = [Scatter(p, wire, part[j], cross_a[j], half_a[j], full_a[j]) for j in range(n)]
    total, root_col, scale, square, cross = (
        Column(cols, i, size) for i, size in enumerate((8 * tok, 8 * tok, slots, tok, tok))
    )
    where = [(s, c) for c in (False, True) for s in range(4) if s or c]

    def everyone(table):
        reserved = [wire.reserve() for _ in where]

        def begin():
            for slot, (step, core) in zip(reserved, where):
                wire.start(slot, table.at[p.t], table.at[p.t], (p.e, p.column(step, core)))

        def settle():
            for slot, (step, core) in zip(reserved, where):
                wire.arrived(slot, table.at[p.column(-step, core)])

        return begin, settle

    info_begin, info_settle = everyone(info)
    roots_begin, roots_settle = everyone(roots)
    slopes_begin, slopes_settle = everyone(slopes)

    def exchanges(kind, src, dst):
        return [
            Exchange(p, src[j], dst[j], *(plane_sems.at[kind * n + j, i] for i in range(3)))
            for j in range(n)
        ]

    swap_g = exchanges(0, rows_a, land_g)
    swap_n = exchanges(1, rows_b, rows_c)
    swap_o = exchanges(2, rows_b, land_o)
    swap_b = exchanges(3, rows_c, land_b)
    swap_r = Exchange(p, root_out, root_in, *(plane_sems.at[4 * n, i] for i in range(3)))
    own_rows = pl.ds(pl.multiple_of(p.t * tok, tok), tok)

    def load(src, dst, j, kind):
        return pltpu.make_async_copy(src, dst, load_sems.at[j, kind])

    def row_block(index, size):
        return pl.ds(pl.multiple_of(index * size, size), size)

    span = 8 * group
    pair = 2 * tok
    depth = act.shape[2]
    tiles = inner // depth
    halves = range(slots // span)

    def peers(b):
        return pl.ds(b * 8, 8)

    def pre_rows(i, b):
        return pl.ds(pl.multiple_of(i * slots + b * span, span), span)

    def column(row):
        return jnp.broadcast_to(row, (tok, tok)).T[:, :1]

    def gain_of(j):
        at, w = cuts[j]
        return gain[:, at : at + w].astype(F32)

    def part_store(ref, quarter, at, size, value):
        ref[row_block(quarter, tok), at : at + size] = value[:tok]
        ref[row_block(4 + quarter, tok), at : at + size] = value[tok:]


    def begin_grads(j):
        gather_g[j].begin()

    def project(j):
        at_j, w = cuts[j]
        load(proj_t.at[pl.ds(at_j, w)], proj.at[pl.ds(at_j, w)], j, 0).wait()

        @pl.loop(0, 4)
        def _(quarter):
            lhs = ctx[row_block(quarter, pair), :]
            for at, size in tiles_of(w):
                got = dot_nt(lhs, proj[at_j + at : at_j + at + size, :]).astype(BF16)
                part_store(part[j], quarter, at, size, got)

        sum_a[j].begin()

    def choices():
        info_settle()

        @pl.loop(0, slots // 80)
        def _(block):
            first = block * 80 + p.t * slots
            slot_id = (lax.broadcasted_iota(jnp.int32, (80, tok), 0) + first).astype(F32)
            rows = row_block(block, 80)
            weight = jnp.zeros((80, tok), F32)
            for s in range(8):
                facts = info[s]
                whole = facts[4:5] + facts[5:6] + facts[6:7] + facts[7:8]
                hits = jnp.zeros((80, tok), F32)
                for k in range(4):
                    hit = slot_id == facts[k : k + 1]
                    hits = jnp.where(hit, 1.0, hits)
                    weight = jnp.where(hit, facts[4 + k : 5 + k] / whole, weight)
                maps[rows, s * tok : (s + 1) * tok] = hits.astype(BF16)
            scale[rows, :] = jnp.sum(weight, axis=1, keepdims=True)

    def select(j, table, out, weighted):
        @pl.loop(0, slots // span)
        def _(b):
            lhs = maps[row_block(b, span), : 8 * tok]
            for at, size in tiles_of(cuts[j][1]):
                rhs = table[: 8 * tok, at : at + size]
                got = jnp.dot(lhs, rhs, preferred_element_type=F32)
                if weighted:
                    got = got * scale[row_block(b, span), :]
                out[peers(b), :, at : at + size] = got.reshape(8, group, size).astype(BF16)

    def send_grads(j):
        gather_g[j].settle()
        select(j, up[j], rows_a[j], True)
        swap_g[j].begin()

    def project_back(j, table, first, scaled):
        at_j, w = cuts[j]

        @pl.loop(0, 4)
        def _(quarter):
            lhs = table[row_block(quarter, pair), :]
            if scaled:
                lhs = (lhs.astype(F32) * (1.0 / gain_of(j))).astype(BF16)
            value = jnp.dot(lhs, proj[at_j : at_j + w, :], preferred_element_type=F32)
            rows = row_block(first * 4 + quarter, pair)
            pre[rows, :] = value if j == 0 else pre[rows, :] + value

    def grads_back(j):
        project_back(j, up[j], 0, False)
        wire.drain(gather_g[j].slots)
        at, w = cuts[j]
        load(up_t.at[:, pl.ds(at, w)], up[j], j, 1).start()

    def hidden_chunk(j):
        at, w = cuts[j]
        sum_a[j].settle()
        value = res_t[at : at + w, :].astype(F32).T + sum_a[j].value()
        hidden[:, at : at + w] = value
        low[j][own_rows, :] = (value * gain_of(j)).astype(BF16)
        gather_n[j].begin()
        here = jnp.sum(value * value, axis=1, keepdims=True)
        square[...] = here if j == 0 else square[...] + here

    def root():
        inv = lax.rsqrt(square[...] / width + 1e-05)
        square[...] = inv
        roots[p.t] = jnp.broadcast_to(inv, (tok, tok)).T[:8]
        roots_begin()

    def send_roots():
        roots_settle()
        for s in range(8):
            root_col[s * tok : (s + 1) * tok, :] = column(roots[s][0:1])

        @pl.loop(0, slots // 80)
        def _(block):
            value = jnp.zeros((80, tok), F32)
            for s in range(8):
                hits = maps[row_block(block, 80), s * tok : (s + 1) * tok].astype(F32)
                value += hits * roots[s][0:1]
            value = jnp.sum(value, axis=1, keepdims=True)
            wide = jnp.broadcast_to(value, (80, tok)).reshape(80 // group, group, tok)
            root_out[pl.ds(block * (80 // group), 80 // group)] = wide

        swap_r.begin()

    def send_rows(j):
        gather_n[j].settle()
        select(j, low[j], rows_b[j], False)
        swap_n[j].begin()

    def rows_back(j):
        project_back(j, low[j], 1, True)
        wire.drain(gather_n[j].slots)
        at, w = cuts[j]
        load(down.at[:, pl.ds(at, w)], low[j], j, 2).start()

    def park_out():
        load(pre, park, n, 0).start()

    def picks():
        @pl.loop(0, 8)
        def _(s):
            facts = jnp.concatenate([info[s], jnp.zeros((tok - 8, tok), F32)], axis=0).T
            slot_id = (lax.broadcasted_iota(jnp.int32, (tok, slots), 1) + p.t * slots).astype(F32)
            hits = jnp.zeros((tok, slots), F32)
            taken = jnp.zeros((tok, slots), F32)
            for k in range(4):
                hit = slot_id == facts[:, k : k + 1]
                hits = jnp.where(hit, 1.0, hits)
                taken = jnp.where(hit, facts[:, 4 + k : 5 + k], taken)
            rows = row_block(s, tok)
            maps[rows, :slots] = hits.astype(BF16)
            maps[rows, slots:] = taken.astype(BF16)
            total[rows, :] = facts[:, 4:5] + facts[:, 5:6] + facts[:, 6:7] + facts[:, 7:8]

    def forward():
        load(pre, park, n, 0).wait()
        for j, (at, w) in enumerate(cuts):
            load(up_t.at[:, pl.ds(at, w)], up[j], j, 1).wait()
            swap_n[j].arrived()
            swap_n[j].drain()
        swap_r.arrived()
        swap_r.drain()

        @pl.loop(0, tiles)
        def _(i):
            @pl.loop(0, slots // span)
            def _(b):
                value = sum(
                    dot_nt(
                        rows_c[j][peers(b)].reshape(span, cuts[j][1]), up[j][row_block(i, depth), :]
                    )
                    for j in range(n)
                )
                value = value * root_in[peers(b)].reshape(span, tok)[:, :1]
                pre[pre_rows(i, b), :depth] = value
                act[i, row_block(b, span), :] = (value / (1.0 + jnp.exp(-value))).astype(BF16)

    def widen(weight, j, out):
        @pl.loop(0, slots // span)
        def _(b):
            for at, size in tiles_of(cuts[j][1]):
                value = sum(
                    jnp.dot(
                        act[i, row_block(b, span), :],
                        weight[j][i * depth : (i + 1) * depth, at : at + size],
                        preferred_element_type=F32,
                    )
                    for i in range(tiles)
                )
                out[peers(b), :, at : at + size] = value.reshape(8, group, size).astype(BF16)

    def expert_out(j):
        at, w = cuts[j]
        load(down.at[:, pl.ds(at, w)], low[j], j, 2).wait()
        widen(low, j, rows_b[j])
        swap_o[j].begin()

    def take_grads(j):
        swap_g[j].arrived()
        swap_g[j].drain()
        load(land_g[j], rows_a[j], j, 3).start()

    def backward():
        for j in range(n):
            load(land_g[j], rows_a[j], j, 3).wait()

        @pl.loop(0, tiles)
        def _(i):
            @pl.loop(0, slots // span)
            def _(b):
                value = sum(
                    dot_nt(
                        rows_a[j][peers(b)].reshape(span, cuts[j][1]), low[j][row_block(i, depth), :]
                    )
                    for j in range(n)
                )
                before = pre[pre_rows(i, b), :depth]
                gate = 1.0 / (1.0 + jnp.exp(-before))
                slope = gate * (1.0 + before * (1.0 - gate))
                act[i, row_block(b, span), :] = (value * slope).astype(BF16)

        load(park, pre, n, 1).start()

    def expert_grad(j):
        widen(up, j, rows_c[j])
        swap_b[j].begin()

    def take_out(j):
        swap_o[j].arrived()
        load(land_o[j], rows_a[j], j, 4).start()

    def take_back(j):
        swap_o[j].drain()
        swap_b[j].arrived()
        load(land_b[j], rows_b[j], j, 5).start()

    def combine(j, first, rows, ref, shared):
        @pl.loop(0, 4)
        def _(quarter):
            lhs = maps[row_block(quarter, pair), first : first + slots]
            for at, size in tiles_of(cuts[j][1]):
                rhs = rows[:, :, at : at + size].reshape(slots, size)
                value = jnp.dot(lhs, rhs, preferred_element_type=F32)
                if shared:
                    value = value / total[row_block(quarter, pair), :]
                part_store(ref, quarter, at, size, value.astype(BF16))

    def mix_chunk(j):
        load(land_o[j], rows_a[j], j, 4).wait()
        combine(j, slots, rows_a[j], low[j], True)
        sum_o[j].begin()

    def grad_chunk(j):
        load(land_b[j], rows_b[j], j, 5).wait()
        sum_a[j].release()
        combine(j, 0, rows_b[j], part[j], False)
        sum_g[j].begin()

    def mixed_out(j):
        at, w = cuts[j]
        sum_o[j].settle()
        mixed_t[at : at + w, :] = (hidden[:, at : at + w] + sum_o[j].value()).T.astype(BF16)

    def scaled_grad(j):
        at, w = cuts[j]
        sum_g[j].settle()
        scaled = sum_g[j].value() * gain_of(j)
        up[j][own_rows, :] = scaled.astype(BF16)
        gather_r[j].begin()
        here = jnp.sum(hidden[:, at : at + w] * scaled, axis=1, keepdims=True)
        cross[...] = here if j == 0 else cross[...] + here

    def slope_out():
        inv = square[...]
        cross[...] = inv * inv * inv * (cross[...] / width)
        slopes[p.t] = jnp.broadcast_to(cross[...], (tok, tok)).T[:8]
        slopes_begin()

    def residual_out():
        for j, (at, w) in enumerate(cuts):
            scaled = sum_g[j].value() * gain_of(j)
            value = square[...] * scaled - hidden[:, at : at + w] * cross[...]
            residual_t[at : at + w, :] = (grad_t[at : at + w, :].astype(F32) + value.T).astype(BF16)

    def accumulate(j):
        if j == 0:
            load(park, pre, n, 1).wait()
        gather_r[j].settle()
        at, w = cuts[j]

        @pl.loop(0, 4)
        def _(quarter):
            rows = row_block(quarter, pair)
            value = jnp.dot(up[j][rows, :], proj[at : at + w, :], preferred_element_type=F32)
            pre[rows, :] = pre[rows, :] + value * root_col[rows, :]

    def context_out():
        slopes_settle()

        @pl.loop(0, 8)
        def _(s):
            rows = row_block(s, tok)
            value = pre[rows, :] - pre[row_block(8 + s, tok), :] * column(slopes[s][0:1])
            grad_context[rows, :] = value.astype(BF16)

    by_chunk = {"ggB": begin_grads, "P": project, "SG": send_grads, "G": grads_back}
    by_chunk |= {"H": hidden_chunk, "SN": send_rows, "N": rows_back, "O": expert_out}
    by_chunk |= {"CT": take_grads, "B": expert_grad, "LO": take_out, "LB": take_back}
    by_chunk |= {"CO": mix_chunk, "CB": grad_chunk, "MX": mixed_out, "Q": scaled_grad}
    by_chunk["AC"] = accumulate
    for name, gathers in (("gg", gather_g), ("gn", gather_n), ("gr", gather_r)):
        by_chunk[name + "F"] = lambda j, of=gathers: of[j].forward()
        by_chunk[name + "E"] = lambda j, of=gathers: of[j].finish()
    for name, sums in (("sa", sum_a), ("so", sum_o), ("sg", sum_g)):
        by_chunk[name + "C"] = lambda j, of=sums: of[j].cores()
        by_chunk[name + "A"] = lambda j, of=sums: of[j].around()
    once = {"CH": choices, "R": root, "RS": send_roots, "PK": picks, "PARK": park_out}
    once |= {"FWD": forward, "BH": backward, "M": slope_out, "RES": residual_out}
    once["END"] = context_out

    load(context, ctx, n, 2).start()
    for j, (at, w) in enumerate(cuts):
        load(proj_t.at[pl.ds(at, w)], proj.at[pl.ds(at, w)], j, 0).start()
    for j, (at, w) in enumerate(cuts):
        up[j][own_rows, :] = grad_t[at : at + w, :].astype(F32).T.astype(BF16)

    experts = 128
    which = lax.broadcasted_iota(jnp.int32, (experts, tok), 0)
    route = [ids[k : k + 1, :] for k in range(4)]
    named = sum((which == r).astype(F32) for r in route)
    before = (
        lax.broadcasted_iota(jnp.int32, (tok, tok), 0)
        < lax.broadcasted_iota(jnp.int32, (tok, tok), 1)
    ).astype(BF16)
    earlier = jnp.dot(named.astype(BF16), before, preferred_element_type=F32)
    codes = []
    for r in route:
        rank = jnp.sum(jnp.where(which == r, earlier, 0.0), axis=0, keepdims=True)
        place = jnp.bitwise_and(r, 7) * slots + jnp.right_shift(r, 3) * group + p.t * CAP
        codes.append(place.astype(F32) + rank)
    info[p.t] = jnp.concatenate(codes + [counts[...].astype(F32)], axis=0)
    greet(p)
    info_begin()
    load(context, ctx, n, 2).wait()

    for step in ORDER:
        name = step.rstrip("0123456789")
        if name == step:
            once[name]()
        else:
            by_chunk[name](int(step[len(name) :]))

    for swapped in swap_b:
        swapped.drain()
    wire.drain()


def whole_block(
    context, proj_t, res_t, gain, ids, counts, grad_t, up_t, down, n_expert, n_tensor
):
    width, tok = res_t.shape
    inner = down.shape[0]
    depth = proj_t.shape[1]
    group = n_tensor * CAP
    slots = n_expert * group
    cuts = chunks_of(width)
    n = len(cuts)
    tiles = 3
    hbm = pl.BlockSpec(memory_space=pl.ANY)
    vmem = pl.BlockSpec(memory_space=pltpu.VMEM)
    landing = [jax.ShapeDtypeStruct((n_expert, group, w), BF16) for _, w in cuts]
    per = lambda *lead: [pltpu.VMEM(lead + (w,), BF16) for _, w in cuts]
    small = pltpu.VMEM((n_tensor, 8, tok), F32)
    copies = (3 * 8 + 3 * 5) * n + 3 * 7
    work_rows = max(tiles * slots, 2 * n_tensor * tok)
    outs = pl.pallas_call(
        functools.partial(kernel, (tok, width, group, slots, inner)),
        out_shape=(
            jax.ShapeDtypeStruct((width, tok), BF16),
            jax.ShapeDtypeStruct((width, tok), BF16),
            jax.ShapeDtypeStruct((n_tensor * tok, depth), BF16),
            jax.ShapeDtypeStruct((work_rows, depth), F32),
            *landing * 3,
        ),
        in_specs=[hbm, hbm] + [vmem] * 5 + [hbm, hbm],
        out_specs=tuple([vmem] * 3 + [hbm] * (1 + 3 * n)),
        scratch_shapes=per(n_expert, group) * 3
        + per(inner) * 2
        + [
            pltpu.VMEM((width, depth), BF16),
            pltpu.VMEM((tok, width), F32),
            small,
            pltpu.VMEM((work_rows, depth), F32),
            pltpu.VMEM((tiles, slots, inner // tiles), BF16),
            pltpu.VMEM((n_tensor * tok, 2 * slots), BF16),
            pltpu.VMEM((n_tensor * tok, 128), F32),
            small,
            pltpu.VMEM((n_expert, group, tok), F32),
            pltpu.VMEM((n_expert, group, tok), F32),
            small,
        ]
        + per(n_tensor * tok)
        + (per(4 * tok) + per(2, tok // 2) + per(2, tok)) * 2
        + [
            pltpu.SemaphoreType.DMA((copies,)),
            pltpu.SemaphoreType.DMA((copies,)),
            pltpu.SemaphoreType.DMA((n + 1, 6)),
            pltpu.SemaphoreType.DMA((4 * n + 1, 3)),
        ],
        compiler_params=pltpu.CompilerParams(
            collective_id=1, has_side_effects=True, vmem_limit_bytes=VMEM_LIMIT
        ),
        name="whole_block",
    )(context, proj_t, res_t, gain, ids, counts, grad_t, up_t, down)
    return outs[0].T, outs[1].T, outs[2]


def local(
    context, out_proj, residual_in, gain, up_weight, down_weight, expert_ids, gate_counts, grad_out
):
    return whole_block(
        context, out_proj.T, residual_in.T, gain.reshape(1, -1), expert_ids.T, gate_counts.T,
        grad_out.T, up_weight[0].T, down_weight[0], lax.axis_size("expert"), lax.axis_size("tensor"),
    )


def solution(mesh):
    whole = P(("expert", "tensor"), None)
    in_specs = (
        P("expert", "tensor"),
        P("tensor", None),
        whole,
        P(),
        P(("expert", "tensor"), None, None),
        P(("expert", "tensor"), None, None),
        whole,
        whole,
        whole,
    )
    out_specs = (whole, whole, P("expert", "tensor"))
    return jax.shard_map(local, mesh=mesh, in_specs=in_specs, out_specs=out_specs, check_vma=False)
```

```python
import functools
import math

import jax
import jax.numpy as jnp
from jax import lax
from jax.experimental import pallas as pl
from jax.experimental.pallas import tpu as pltpu
from jax.sharding import PartitionSpec as P

CAP = 5
STARTS = (0, 512, 1024, 1792, 2432)
MESH = pl.DeviceIdType.MESH
F32, BF16 = jnp.float32, jnp.bfloat16
VMEM_LIMIT = 65000 * 2**10


def chunks_of(width):
    starts = STARTS + (width,)
    return [(at, end - at) for at, end in zip(starts, starts[1:])]


def dot_nt(a, b):
    return lax.dot_general(a, b, (((1,), (1,)), ((), ())), preferred_element_type=F32)


def tiles_of(width, step=512):
    return [(at, min(step, width - at)) for at in range(0, width, step)]


PLANE = [
    (0, 1), (1, 0), (0, 3), (3, 0), (1, 1), (3, 3), (1, 3), (3, 1),
    (0, 2), (2, 0), (1, 2), (2, 1), (3, 2), (2, 3), (2, 2),
]


class Place:
    def __init__(self):
        self.e, self.t = lax.axis_index("expert"), lax.axis_index("tensor")
        self.x, self.c = self.t // 2, lax.rem(self.t, 2)
        self.z, self.y = self.e // 4, lax.rem(self.e, 4)

    def column(self, step, other=False):
        core = 1 - self.c if other else self.c
        return lax.rem(self.x + step + 4, 4) * 2 + core

    def plane(self, offset):
        return lax.rem(self.z + offset[0], 4) * 4 + lax.rem(self.y + offset[1], 4)


class Wire:
    def __init__(self, send_sems, recv_sems):
        self.send_sems, self.recv_sems, self.count, self.sent = send_sems, recv_sems, 0, []

    def reserve(self):
        self.count += 1
        return self.count - 1

    def start(self, slot, src, dst, dev):
        copy = pltpu.make_async_remote_copy(
            src, dst, self.send_sems.at[slot], self.recv_sems.at[slot],
            device_id=dev, device_id_type=MESH,
        )
        copy.start()
        self.sent.append((slot, copy))

    def arrived(self, slot, landing):
        pltpu.make_async_copy(landing, landing, self.recv_sems.at[slot]).wait()

    def drain(self, slots=None):
        for slot, copy in self.sent:
            if slots is None or slot in slots:
                copy.wait_send()
        self.sent = [] if slots is None else [item for item in self.sent if item[0] not in slots]


class Gather:
    def __init__(self, place, wire, table, rows):
        self.p, self.w, self.table, self.rows = place, wire, table, rows
        self.slots = [wire.reserve() for _ in range(8)]

    def block(self, index, half=None):
        size = self.rows if half is None else self.rows // 2
        first = index * self.rows + (half or 0) * size
        return self.table.at[pl.ds(pl.multiple_of(first, size), size)]

    def begin(self):
        p, w, s = self.p, self.w, self.slots
        own = self.block(p.t)
        w.start(s[0], own, own, (p.e, p.column(1)))
        w.start(s[1], own, own, (p.e, p.column(-1)))
        w.start(s[2], own, own, (p.e, p.column(0, True)))

    def forward(self):
        p, w, s = self.p, self.w, self.slots
        left, right = self.block(p.column(-1)), self.block(p.column(1))
        partner = (p.e, p.column(0, True))
        w.arrived(s[0], left)
        near = self.block(p.column(-1), 0)
        w.start(s[3], near, near, (p.e, p.column(1)))
        w.start(s[5], left, left, partner)
        w.arrived(s[1], right)
        near = self.block(p.column(1), 1)
        w.start(s[4], near, near, (p.e, p.column(-1)))
        w.start(s[6], right, right, partner)

    def finish(self):
        p, w, s = self.p, self.w, self.slots
        far = self.block(p.column(2))
        w.arrived(s[3], self.block(p.column(2), 0))
        w.arrived(s[4], self.block(p.column(2), 1))
        w.start(s[7], far, far, (p.e, p.column(0, True)))

    def settle(self):
        p, w, s = self.p, self.w, self.slots
        for slot, step in ((s[2], 0), (s[5], -1), (s[6], 1), (s[7], 2)):
            w.arrived(slot, self.block(p.column(step, True)))


class Scatter:
    def __init__(self, place, wire, part, cross, half, full):
        self.p, self.w = place, wire
        self.part, self.cross, self.half, self.full = part, cross, half, full
        self.slots = [wire.reserve() for _ in range(5)]
        self.rows = full.shape[1]

    def at(self, core, x, half=None):
        size = self.rows if half is None else self.rows // 2
        first = (core * 4 + x) * self.rows + (half or 0) * size
        return pl.ds(pl.multiple_of(first, size), size)

    def begin(self):
        p = self.p
        theirs = pl.ds(pl.multiple_of((1 - p.c) * 4 * self.rows, 4 * self.rows), 4 * self.rows)
        self.w.start(self.slots[0], self.part.at[theirs], self.cross, (p.e, p.column(0, True)))

    def cores(self):
        p, w, s = self.p, self.w, self.slots
        w.arrived(s[0], self.cross)
        far = lax.rem(p.x + 2, 4)

        def add(x):
            rows = self.at(p.c, x)
            theirs = pl.ds(pl.multiple_of(x * self.rows, self.rows), self.rows)
            mine = self.part[rows, :].astype(F32)
            self.part[rows, :] = (mine + self.cross[theirs, :].astype(F32)).astype(BF16)

        add(far)
        w.start(s[1], self.part.at[self.at(p.c, far, 0)], self.half.at[0], (p.e, p.column(1)))
        w.start(s[2], self.part.at[self.at(p.c, far, 1)], self.half.at[1], (p.e, p.column(-1)))
        add(lax.rem(p.x + 1, 4))
        add(lax.rem(p.x + 3, 4))
        add(p.x)

    def around(self):
        p, w, s = self.p, self.w, self.slots
        for side, step in ((0, 1), (1, -1)):
            x = lax.rem(p.x + step + 4, 4)
            w.arrived(s[1 + side], self.half.at[side])
            rows = self.at(p.c, x, side)
            mine = self.part[rows, :].astype(F32)
            self.part[rows, :] = (mine + self.half[side].astype(F32)).astype(BF16)
            w.start(
                s[3 + side], self.part.at[self.at(p.c, x)], self.full.at[side],
                (p.e, p.column(step)),
            )

    def settle(self):
        self.w.arrived(self.slots[3], self.full.at[0])
        self.w.arrived(self.slots[4], self.full.at[1])

    def value(self):
        total = self.part[self.at(self.p.c, self.p.x), :].astype(F32)
        return total + self.full[0].astype(F32) + self.full[1].astype(F32)

    def release(self):
        self.w.drain(self.slots)


class Exchange:
    def __init__(self, place, src, dst, send_sem, recv_sem, own_sem):
        self.p, self.src, self.dst = place, src, dst
        self.sems = (send_sem, recv_sem, own_sem)

    def begin(self):
        p = self.p
        send_sem, recv_sem, own_sem = self.sems
        for offset in PLANE:
            peer = p.plane(offset)
            pltpu.make_async_remote_copy(
                self.src.at[peer], self.dst.at[p.e], send_sem, recv_sem,
                device_id=(peer, p.t), device_id_type=MESH,
            ).start()
        pltpu.make_async_copy(self.src.at[p.e], self.dst.at[p.e], own_sem).start()

    def arrived(self):
        p = self.p
        others = self.dst.at[pl.ds(0, len(PLANE))]
        pltpu.make_async_copy(others, others, self.sems[1]).wait()
        pltpu.make_async_copy(self.src.at[p.e], self.dst.at[p.e], self.sems[2]).wait()

    def drain(self):
        others = self.src.at[pl.ds(0, len(PLANE))]
        pltpu.make_async_copy(others, others, self.sems[0]).wait()


def greet(place):
    barrier = pltpu.get_barrier_semaphore()
    count = 0
    for core in (False, True):
        for step in range(4):
            if step or core:
                dev = (place.e, place.column(step, core))
                pl.semaphore_signal(barrier, inc=1, device_id=dev, device_id_type=MESH)
                count += 1
    for offset in PLANE:
        dev = (place.plane(offset), place.t)
        pl.semaphore_signal(barrier, inc=1, device_id=dev, device_id_type=MESH)
        count += 1
    pl.semaphore_wait(barrier, count)


ORDER = (
    "ggB0", "ggB1", "P0", "P1", "ggF0", "CH", "saC0", "ggF1", "ggE0", "ggB2",
    "saA0", "SG0", "ggE1", "saC1", "P2", "SG1", "ggF2", "P3", "H0", "ggE2",
    "saC2", "G0", "saA1", "SG2", "gnF0", "saA2", "H1", "gnE0", "H2", "SN0",
    "gnF1", "saC3", "N0", "P4", "G1", "gnF2", "gnE1", "saA3", "SN1", "N1",
    "saC4", "gnE2", "G2", "H3", "saA4", "SN2", "N2", "gnF3", "H4", "gnE3",
    "ggB3", "R", "gnF4", "SN3", "ggB4", "ggF3", "gnE4", "RS", "SN4", "ggF4",
    "ggE3", "N3", "N4", "ggE4", "SG3", "SG4", "G3", "G4", "PARK", "FWD",
    "O0", "O1", "CT1", "OS0", "CT0", "O2", "CT3", "O3", "OS1", "CT4",
    "O4", "CT2", "BH", "B0", "B1", "LO0", "LO1", "PK", "CO0", "CO1",
    "B2", "LB0", "soC0", "soC1", "CB0", "soA0", "LB1", "sgC0", "CB1", "soA1",
    "B3", "sgA0", "B4", "sgC1", "Q0", "LB2", "sgA1", "CB2", "OS2", "grF0",
    "MX1", "sgC2", "Q1", "grE0", "LB3", "sgA2", "CB3", "grF1", "sgC3", "LB4",
    "OS3", "Q2", "sgA3", "CB4", "MX0", "grF2", "OS4", "sgC4", "LO2", "Q3",
    "CO2", "sgA4", "soC2", "LO3", "grF3", "AC0", "grE2", "Q4", "CO3", "M",
    "soA2", "LO4", "soC3", "grE1", "CO4", "grE3", "grF4", "soC4", "MX2", "soA3",
    "AC1", "grE4", "soA4", "AC2", "AC3", "MX3", "AC4", "RES", "MX4", "END",
)


class Column:
    def __init__(self, ref, index, size):
        self.ref, self.index, self.size = ref, index, size

    def rows(self, key):
        if key is Ellipsis:
            return pl.ds(0, self.size)
        return key[0]

    def __getitem__(self, key):
        return self.ref[self.rows(key), self.index : self.index + 1]

    def __setitem__(self, key, value):
        self.ref[self.rows(key), self.index : self.index + 1] = value


def kernel(dims, *refs):
    tok, width, group, slots, inner = dims
    cuts = chunks_of(width)
    n = len(cuts)
    refs = list(refs)

    def take(k):
        out = refs[:k]
        del refs[:k]
        return out

    context, proj_t, res_t, gain, ids, counts, grad_t, up_t, down = take(9)
    mixed_t, residual_t, grad_context, park = take(4)
    land_g, land_o, land_b = take(n), take(n), take(n)
    rows_a, rows_b, rows_c = take(n), take(n), take(n)
    up, low = take(n), take(n)
    proj, hidden, info, pre, act, maps, cols = take(7)
    roots, root_out, root_in, slopes = take(4)
    part = take(n)
    cross_a, half_a, full_a = take(n), take(n), take(n)
    cross_b, half_b, full_b = take(n), take(n), take(n)
    send_sems, recv_sems, load_sems, plane_sems = refs

    p = Place()
    ctx = grad_context
    wire = Wire(send_sems, recv_sems)
    gather_g = [Gather(p, wire, up[j], tok) for j in range(n)]
    gather_n = [Gather(p, wire, low[j], tok) for j in range(n)]
    gather_r = [Gather(p, wire, up[j], tok) for j in range(n)]
    sum_a = [Scatter(p, wire, part[j], cross_a[j], half_a[j], full_a[j]) for j in range(n)]
    sum_o = [Scatter(p, wire, low[j], cross_b[j], half_b[j], full_b[j]) for j in range(n)]
    sum_g = [Scatter(p, wire, part[j], cross_a[j], half_a[j], full_a[j]) for j in range(n)]
    total, root_col, scale, square, cross = (
        Column(cols, i, size) for i, size in enumerate((8 * tok, 8 * tok, slots, tok, tok))
    )
    where = [(s, c) for c in (False, True) for s in range(4) if s or c]

    def everyone(table):
        reserved = [wire.reserve() for _ in where]

        def begin():
            for slot, (step, core) in zip(reserved, where):
                wire.start(slot, table.at[p.t], table.at[p.t], (p.e, p.column(step, core)))

        def settle():
            for slot, (step, core) in zip(reserved, where):
                wire.arrived(slot, table.at[p.column(-step, core)])

        return begin, settle

    info_begin, info_settle = everyone(info)
    roots_begin, roots_settle = everyone(roots)
    slopes_begin, slopes_settle = everyone(slopes)

    def exchanges(kind, src, dst):
        return [
            Exchange(p, src[j], dst[j], *(plane_sems.at[kind * n + j, i] for i in range(3)))
            for j in range(n)
        ]

    swap_g = exchanges(0, rows_a, land_g)
    swap_n = exchanges(1, rows_b, rows_c)
    swap_o = exchanges(2, rows_b, land_o)
    swap_b = exchanges(3, rows_c, land_b)
    swap_r = Exchange(p, root_out, root_in, *(plane_sems.at[4 * n, i] for i in range(3)))
    own_rows = pl.ds(pl.multiple_of(p.t * tok, tok), tok)

    def load(src, dst, j, kind):
        return pltpu.make_async_copy(src, dst, load_sems.at[j, kind])

    def row_block(index, size):
        return pl.ds(pl.multiple_of(index * size, size), size)

    span = 8 * group
    pair = 2 * tok
    depth = act.shape[2]
    tiles = inner // depth
    halves = range(slots // span)

    def peers(b):
        return pl.ds(b * 8, 8)

    def pre_rows(i, b):
        return pl.ds(pl.multiple_of(i * slots + b * span, span), span)

    def column(row):
        return jnp.broadcast_to(row, (tok, tok)).T[:, :1]

    def gain_of(j):
        at, w = cuts[j]
        return gain[:, at : at + w].astype(F32)

    def part_store(ref, quarter, at, size, value):
        ref[row_block(quarter, tok), at : at + size] = value[:tok]
        ref[row_block(4 + quarter, tok), at : at + size] = value[tok:]


    def begin_grads(j):
        gather_g[j].begin()

    def project(j):
        at_j, w = cuts[j]
        load(proj_t.at[pl.ds(at_j, w)], proj.at[pl.ds(at_j, w)], j, 0).wait()

        @pl.loop(0, 4)
        def _(quarter):
            lhs = ctx[row_block(quarter, pair), :]
            for at, size in tiles_of(w):
                got = dot_nt(lhs, proj[at_j + at : at_j + at + size, :]).astype(BF16)
                part_store(part[j], quarter, at, size, got)

        sum_a[j].begin()

    def choices():
        info_settle()

        @pl.loop(0, slots // 80)
        def _(block):
            first = block * 80 + p.t * slots
            slot_id = (lax.broadcasted_iota(jnp.int32, (80, tok), 0) + first).astype(F32)
            rows = row_block(block, 80)
            weight = jnp.zeros((80, tok), F32)
            for s in range(8):
                facts = info[s]
                whole = facts[4:5] + facts[5:6] + facts[6:7] + facts[7:8]
                hits = jnp.zeros((80, tok), F32)
                for k in range(4):
                    hit = slot_id == facts[k : k + 1]
                    hits = jnp.where(hit, 1.0, hits)
                    weight = jnp.where(hit, facts[4 + k : 5 + k] / whole, weight)
                maps[rows, s * tok : (s + 1) * tok] = hits.astype(BF16)
            scale[rows, :] = jnp.sum(weight, axis=1, keepdims=True)

    def select(j, table, out, weighted):
        @pl.loop(0, slots // span)
        def _(b):
            lhs = maps[row_block(b, span), : 8 * tok]
            for at, size in tiles_of(cuts[j][1]):
                rhs = table[: 8 * tok, at : at + size]
                got = jnp.dot(lhs, rhs, preferred_element_type=F32)
                if weighted:
                    got = got * scale[row_block(b, span), :]
                out[peers(b), :, at : at + size] = got.reshape(8, group, size).astype(BF16)

    def send_grads(j):
        gather_g[j].settle()
        select(j, up[j], rows_a[j], True)
        swap_g[j].begin()

    def project_back(j, table, first, scaled):
        at_j, w = cuts[j]

        @pl.loop(0, 4)
        def _(quarter):
            lhs = table[row_block(quarter, pair), :]
            if scaled:
                lhs = (lhs.astype(F32) * (1.0 / gain_of(j))).astype(BF16)
            value = jnp.dot(lhs, proj[at_j : at_j + w, :], preferred_element_type=F32)
            rows = row_block(first * 4 + quarter, pair)
            pre[rows, :] = value if j == 0 else pre[rows, :] + value

    def grads_back(j):
        project_back(j, up[j], 0, False)
        wire.drain(gather_g[j].slots)
        at, w = cuts[j]
        load(up_t.at[:, pl.ds(at, w)], up[j], j, 1).start()

    def hidden_chunk(j):
        at, w = cuts[j]
        sum_a[j].settle()
        value = res_t[at : at + w, :].astype(F32).T + sum_a[j].value()
        hidden[:, at : at + w] = value
        low[j][own_rows, :] = (value * gain_of(j)).astype(BF16)
        gather_n[j].begin()
        here = jnp.sum(value * value, axis=1, keepdims=True)
        square[...] = here if j == 0 else square[...] + here

    def root():
        inv = lax.rsqrt(square[...] / width + 1e-05)
        square[...] = inv
        roots[p.t] = jnp.broadcast_to(inv, (tok, tok)).T[:8]
        roots_begin()

    def send_roots():
        roots_settle()
        for s in range(8):
            root_col[s * tok : (s + 1) * tok, :] = column(roots[s][0:1])

        @pl.loop(0, slots // 80)
        def _(block):
            value = jnp.zeros((80, tok), F32)
            for s in range(8):
                hits = maps[row_block(block, 80), s * tok : (s + 1) * tok].astype(F32)
                value += hits * roots[s][0:1]
            value = jnp.sum(value, axis=1, keepdims=True)
            wide = jnp.broadcast_to(value, (80, tok)).reshape(80 // group, group, tok)
            root_out[pl.ds(block * (80 // group), 80 // group)] = wide

        swap_r.begin()

    def send_rows(j):
        gather_n[j].settle()
        select(j, low[j], rows_b[j], False)
        swap_n[j].begin()

    def rows_back(j):
        project_back(j, low[j], 1, True)
        wire.drain(gather_n[j].slots)
        at, w = cuts[j]
        load(down.at[:, pl.ds(at, w)], low[j], j, 2).start()

    def park_out():
        load(pre, park, n, 0).start()

    def picks():
        @pl.loop(0, 8)
        def _(s):
            facts = jnp.concatenate([info[s], jnp.zeros((tok - 8, tok), F32)], axis=0).T
            slot_id = (lax.broadcasted_iota(jnp.int32, (tok, slots), 1) + p.t * slots).astype(F32)
            hits = jnp.zeros((tok, slots), F32)
            taken = jnp.zeros((tok, slots), F32)
            for k in range(4):
                hit = slot_id == facts[:, k : k + 1]
                hits = jnp.where(hit, 1.0, hits)
                taken = jnp.where(hit, facts[:, 4 + k : 5 + k], taken)
            rows = row_block(s, tok)
            maps[rows, :slots] = hits.astype(BF16)
            maps[rows, slots:] = taken.astype(BF16)
            total[rows, :] = facts[:, 4:5] + facts[:, 5:6] + facts[:, 6:7] + facts[:, 7:8]

    def forward():
        load(pre, park, n, 0).wait()
        for j, (at, w) in enumerate(cuts):
            load(up_t.at[:, pl.ds(at, w)], up[j], j, 1).wait()
            swap_n[j].arrived()
            swap_n[j].drain()
        swap_r.arrived()
        swap_r.drain()

        @pl.loop(0, tiles)
        def _(i):
            @pl.loop(0, slots // span)
            def _(b):
                value = sum(
                    dot_nt(
                        rows_c[j][peers(b)].reshape(span, cuts[j][1]), up[j][row_block(i, depth), :]
                    )
                    for j in range(n)
                )
                value = value * root_in[peers(b)].reshape(span, tok)[:, :1]
                pre[pre_rows(i, b), :depth] = value
                act[i, row_block(b, span), :] = (value / (1.0 + jnp.exp(-value))).astype(BF16)

    def widen(weight, j, out):
        @pl.loop(0, slots // span)
        def _(b):
            for at, size in tiles_of(cuts[j][1]):
                value = sum(
                    jnp.dot(
                        act[i, row_block(b, span), :],
                        weight[j][i * depth : (i + 1) * depth, at : at + size],
                        preferred_element_type=F32,
                    )
                    for i in range(tiles)
                )
                out[peers(b), :, at : at + size] = value.reshape(8, group, size).astype(BF16)

    def expert_out(j):
        at, w = cuts[j]
        load(down.at[:, pl.ds(at, w)], low[j], j, 2).wait()
        widen(low, j, rows_b[j])

    def send_out(j):
        swap_o[j].begin()

    def take_grads(j):
        swap_g[j].arrived()
        swap_g[j].drain()
        load(land_g[j], rows_a[j], j, 3).start()

    def backward():
        for j in range(n):
            load(land_g[j], rows_a[j], j, 3).wait()

        @pl.loop(0, tiles)
        def _(i):
            @pl.loop(0, slots // span)
            def _(b):
                value = sum(
                    dot_nt(
                        rows_a[j][peers(b)].reshape(span, cuts[j][1]), low[j][row_block(i, depth), :]
                    )
                    for j in range(n)
                )
                before = pre[pre_rows(i, b), :depth]
                gate = 1.0 / (1.0 + jnp.exp(-before))
                slope = gate * (1.0 + before * (1.0 - gate))
                act[i, row_block(b, span), :] = (value * slope).astype(BF16)

        load(park, pre, n, 1).start()

    def expert_grad(j):
        widen(up, j, rows_c[j])
        swap_b[j].begin()

    def take_out(j):
        swap_o[j].arrived()
        load(land_o[j], rows_a[j], j, 4).start()

    def take_back(j):
        swap_b[j].arrived()
        load(land_b[j], rows_a[j], j, 5).start()

    def combine(j, first, rows, ref, shared):
        @pl.loop(0, 4)
        def _(quarter):
            lhs = maps[row_block(quarter, pair), first : first + slots]
            for at, size in tiles_of(cuts[j][1]):
                rhs = rows[:, :, at : at + size].reshape(slots, size)
                value = jnp.dot(lhs, rhs, preferred_element_type=F32)
                if shared:
                    value = value / total[row_block(quarter, pair), :]
                part_store(ref, quarter, at, size, value.astype(BF16))

    def mix_chunk(j):
        load(land_o[j], rows_a[j], j, 4).wait()
        combine(j, slots, rows_a[j], low[j], True)
        sum_o[j].begin()

    def grad_chunk(j):
        load(land_b[j], rows_a[j], j, 5).wait()
        sum_a[j].release()
        combine(j, 0, rows_a[j], part[j], False)
        sum_g[j].begin()

    def mixed_out(j):
        at, w = cuts[j]
        sum_o[j].settle()
        mixed_t[at : at + w, :] = (hidden[:, at : at + w] + sum_o[j].value()).T.astype(BF16)

    def scaled_grad(j):
        at, w = cuts[j]
        sum_g[j].settle()
        scaled = sum_g[j].value() * gain_of(j)
        up[j][own_rows, :] = scaled.astype(BF16)
        gather_r[j].begin()
        here = jnp.sum(hidden[:, at : at + w] * scaled, axis=1, keepdims=True)
        cross[...] = here if j == 0 else cross[...] + here

    def slope_out():
        inv = square[...]
        cross[...] = inv * inv * inv * (cross[...] / width)
        slopes[p.t] = jnp.broadcast_to(cross[...], (tok, tok)).T[:8]
        slopes_begin()

    def residual_out():
        for j, (at, w) in enumerate(cuts):
            scaled = sum_g[j].value() * gain_of(j)
            value = square[...] * scaled - hidden[:, at : at + w] * cross[...]
            residual_t[at : at + w, :] = (grad_t[at : at + w, :].astype(F32) + value.T).astype(BF16)

    def accumulate(j):
        if j == 0:
            load(park, pre, n, 1).wait()
        gather_r[j].settle()
        at, w = cuts[j]

        @pl.loop(0, 4)
        def _(quarter):
            rows = row_block(quarter, pair)
            value = jnp.dot(up[j][rows, :], proj[at : at + w, :], preferred_element_type=F32)
            pre[rows, :] = pre[rows, :] + value * root_col[rows, :]

    def context_out():
        slopes_settle()

        @pl.loop(0, 8)
        def _(s):
            rows = row_block(s, tok)
            value = pre[rows, :] - pre[row_block(8 + s, tok), :] * column(slopes[s][0:1])
            grad_context[rows, :] = value.astype(BF16)

    by_chunk = {"ggB": begin_grads, "P": project, "SG": send_grads, "G": grads_back}
    by_chunk |= {"H": hidden_chunk, "SN": send_rows, "N": rows_back, "O": expert_out}
    by_chunk |= {"CT": take_grads, "B": expert_grad, "LO": take_out, "LB": take_back}
    by_chunk |= {"CO": mix_chunk, "CB": grad_chunk, "MX": mixed_out, "Q": scaled_grad}
    by_chunk |= {"AC": accumulate, "OS": send_out}
    for name, gathers in (("gg", gather_g), ("gn", gather_n), ("gr", gather_r)):
        by_chunk[name + "F"] = lambda j, of=gathers: of[j].forward()
        by_chunk[name + "E"] = lambda j, of=gathers: of[j].finish()
    for name, sums in (("sa", sum_a), ("so", sum_o), ("sg", sum_g)):
        by_chunk[name + "C"] = lambda j, of=sums: of[j].cores()
        by_chunk[name + "A"] = lambda j, of=sums: of[j].around()
    once = {"CH": choices, "R": root, "RS": send_roots, "PK": picks, "PARK": park_out}
    once |= {"FWD": forward, "BH": backward, "M": slope_out, "RES": residual_out}
    once["END"] = context_out

    load(context, ctx, n, 2).start()
    for j, (at, w) in enumerate(cuts):
        load(proj_t.at[pl.ds(at, w)], proj.at[pl.ds(at, w)], j, 0).start()
    for j, (at, w) in enumerate(cuts):
        up[j][own_rows, :] = grad_t[at : at + w, :].astype(F32).T.astype(BF16)

    experts = 128
    which = lax.broadcasted_iota(jnp.int32, (experts, tok), 0)
    route = [ids[k : k + 1, :] for k in range(4)]
    named = sum((which == r).astype(F32) for r in route)
    before = (
        lax.broadcasted_iota(jnp.int32, (tok, tok), 0)
        < lax.broadcasted_iota(jnp.int32, (tok, tok), 1)
    ).astype(BF16)
    earlier = jnp.dot(named.astype(BF16), before, preferred_element_type=F32)
    codes = []
    for r in route:
        rank = jnp.sum(jnp.where(which == r, earlier, 0.0), axis=0, keepdims=True)
        place = jnp.bitwise_and(r, 7) * slots + jnp.right_shift(r, 3) * group + p.t * CAP
        codes.append(place.astype(F32) + rank)
    info[p.t] = jnp.concatenate(codes + [counts[...].astype(F32)], axis=0)
    greet(p)
    info_begin()
    load(context, ctx, n, 2).wait()

    for step in ORDER:
        name = step.rstrip("0123456789")
        if name == step:
            once[name]()
        else:
            by_chunk[name](int(step[len(name) :]))

    for swapped in swap_o + swap_b:
        swapped.drain()
    wire.drain()


def whole_block(
    context, proj_t, res_t, gain, ids, counts, grad_t, up_t, down, n_expert, n_tensor
):
    width, tok = res_t.shape
    inner = down.shape[0]
    depth = proj_t.shape[1]
    group = n_tensor * CAP
    slots = n_expert * group
    cuts = chunks_of(width)
    n = len(cuts)
    tiles = 3
    hbm = pl.BlockSpec(memory_space=pl.ANY)
    vmem = pl.BlockSpec(memory_space=pltpu.VMEM)
    landing = [jax.ShapeDtypeStruct((n_expert, group, w), BF16) for _, w in cuts]
    per = lambda *lead: [pltpu.VMEM(lead + (w,), BF16) for _, w in cuts]
    small = pltpu.VMEM((n_tensor, 8, tok), F32)
    copies = (3 * 8 + 3 * 5) * n + 3 * 7
    work_rows = max(tiles * slots, 2 * n_tensor * tok)
    outs = pl.pallas_call(
        functools.partial(kernel, (tok, width, group, slots, inner)),
        out_shape=(
            jax.ShapeDtypeStruct((width, tok), BF16),
            jax.ShapeDtypeStruct((width, tok), BF16),
            jax.ShapeDtypeStruct((n_tensor * tok, depth), BF16),
            jax.ShapeDtypeStruct((work_rows, depth), F32),
            *landing * 3,
        ),
        in_specs=[hbm, hbm] + [vmem] * 5 + [hbm, hbm],
        out_specs=tuple([vmem] * 3 + [hbm] * (1 + 3 * n)),
        scratch_shapes=per(n_expert, group) * 3
        + per(inner) * 2
        + [
            pltpu.VMEM((width, depth), BF16),
            pltpu.VMEM((tok, width), F32),
            small,
            pltpu.VMEM((work_rows, depth), F32),
            pltpu.VMEM((tiles, slots, inner // tiles), BF16),
            pltpu.VMEM((n_tensor * tok, 2 * slots), BF16),
            pltpu.VMEM((n_tensor * tok, 128), F32),
            small,
            pltpu.VMEM((n_expert, group, tok), F32),
            pltpu.VMEM((n_expert, group, tok), F32),
            small,
        ]
        + per(n_tensor * tok)
        + (per(4 * tok) + per(2, tok // 2) + per(2, tok)) * 2
        + [
            pltpu.SemaphoreType.DMA((copies,)),
            pltpu.SemaphoreType.DMA((copies,)),
            pltpu.SemaphoreType.DMA((n + 1, 6)),
            pltpu.SemaphoreType.DMA((4 * n + 1, 3)),
        ],
        compiler_params=pltpu.CompilerParams(
            collective_id=1, has_side_effects=True, vmem_limit_bytes=VMEM_LIMIT
        ),
        name="whole_block",
    )(context, proj_t, res_t, gain, ids, counts, grad_t, up_t, down)
    return outs[0].T, outs[1].T, outs[2]


def local(
    context, out_proj, residual_in, gain, up_weight, down_weight, expert_ids, gate_counts, grad_out
):
    return whole_block(
        context, out_proj.T, residual_in.T, gain.reshape(1, -1), expert_ids.T, gate_counts.T,
        grad_out.T, up_weight[0].T, down_weight[0], lax.axis_size("expert"), lax.axis_size("tensor"),
    )


def solution(mesh):
    whole = P(("expert", "tensor"), None)
    in_specs = (
        P("expert", "tensor"),
        P("tensor", None),
        whole,
        P(),
        P(("expert", "tensor"), None, None),
        P(("expert", "tensor"), None, None),
        whole,
        whole,
        whole,
    )
    out_specs = (whole, whole, P("expert", "tensor"))
    return jax.shard_map(local, mesh=mesh, in_specs=in_specs, out_specs=out_specs, check_vma=False)
```

```python
import functools
import math

import jax
import jax.numpy as jnp
from jax import lax
from jax.experimental import pallas as pl
from jax.experimental.pallas import tpu as pltpu
from jax.sharding import PartitionSpec as P

CAP = 5
STARTS = (0, 512, 1024, 1536, 2048, 2560)
MESH = pl.DeviceIdType.MESH
F32, BF16 = jnp.float32, jnp.bfloat16
VMEM_LIMIT = 65000 * 2**10


def chunks_of(width):
    starts = STARTS + (width,)
    return [(at, end - at) for at, end in zip(starts, starts[1:])]


def dot_nt(a, b):
    return lax.dot_general(a, b, (((1,), (1,)), ((), ())), preferred_element_type=F32)


def tiles_of(width, step=512):
    return [(at, min(step, width - at)) for at in range(0, width, step)]


PLANE = [
    (0, 1), (1, 0), (0, 3), (3, 0), (1, 1), (3, 3), (1, 3), (3, 1),
    (0, 2), (2, 0), (1, 2), (2, 1), (3, 2), (2, 3), (2, 2),
]


class Place:
    def __init__(self):
        self.e, self.t = lax.axis_index("expert"), lax.axis_index("tensor")
        self.x, self.c = self.t // 2, lax.rem(self.t, 2)
        self.z, self.y = self.e // 4, lax.rem(self.e, 4)

    def column(self, step, other=False):
        core = 1 - self.c if other else self.c
        return lax.rem(self.x + step + 4, 4) * 2 + core

    def plane(self, offset):
        return lax.rem(self.z + offset[0], 4) * 4 + lax.rem(self.y + offset[1], 4)


class Wire:
    def __init__(self, send_sems, recv_sems):
        self.send_sems, self.recv_sems, self.count, self.sent = send_sems, recv_sems, 0, []

    def reserve(self):
        self.count += 1
        return self.count - 1

    def start(self, slot, src, dst, dev):
        copy = pltpu.make_async_remote_copy(
            src, dst, self.send_sems.at[slot], self.recv_sems.at[slot],
            device_id=dev, device_id_type=MESH,
        )
        copy.start()
        self.sent.append((slot, copy))

    def arrived(self, slot, landing):
        pltpu.make_async_copy(landing, landing, self.recv_sems.at[slot]).wait()

    def drain(self, slots=None):
        for slot, copy in self.sent:
            if slots is None or slot in slots:
                copy.wait_send()
        self.sent = [] if slots is None else [item for item in self.sent if item[0] not in slots]


class Gather:
    def __init__(self, place, wire, table, rows):
        self.p, self.w, self.table, self.rows = place, wire, table, rows
        self.slots = [wire.reserve() for _ in range(8)]

    def block(self, index, half=None):
        size = self.rows if half is None else self.rows // 2
        first = index * self.rows + (half or 0) * size
        return self.table.at[pl.ds(pl.multiple_of(first, size), size)]

    def begin(self):
        p, w, s = self.p, self.w, self.slots
        own = self.block(p.t)
        w.start(s[0], own, own, (p.e, p.column(1)))
        w.start(s[1], own, own, (p.e, p.column(-1)))
        w.start(s[2], own, own, (p.e, p.column(0, True)))

    def forward(self):
        p, w, s = self.p, self.w, self.slots
        left, right = self.block(p.column(-1)), self.block(p.column(1))
        partner = (p.e, p.column(0, True))
        w.arrived(s[0], left)
        near = self.block(p.column(-1), 0)
        w.start(s[3], near, near, (p.e, p.column(1)))
        w.start(s[5], left, left, partner)
        w.arrived(s[1], right)
        near = self.block(p.column(1), 1)
        w.start(s[4], near, near, (p.e, p.column(-1)))
        w.start(s[6], right, right, partner)

    def finish(self):
        p, w, s = self.p, self.w, self.slots
        far = self.block(p.column(2))
        w.arrived(s[3], self.block(p.column(2), 0))
        w.arrived(s[4], self.block(p.column(2), 1))
        w.start(s[7], far, far, (p.e, p.column(0, True)))

    def settle(self):
        p, w, s = self.p, self.w, self.slots
        for slot, step in ((s[2], 0), (s[5], -1), (s[6], 1), (s[7], 2)):
            w.arrived(slot, self.block(p.column(step, True)))


class Scatter:
    def __init__(self, place, wire, part, cross, half, full):
        self.p, self.w = place, wire
        self.part, self.cross, self.half, self.full = part, cross, half, full
        self.slots = [wire.reserve() for _ in range(5)]
        self.rows = full.shape[1]

    def at(self, core, x, half=None):
        size = self.rows if half is None else self.rows // 2
        first = (core * 4 + x) * self.rows + (half or 0) * size
        return pl.ds(pl.multiple_of(first, size), size)

    def begin(self):
        p = self.p
        theirs = pl.ds(pl.multiple_of((1 - p.c) * 4 * self.rows, 4 * self.rows), 4 * self.rows)
        self.w.start(self.slots[0], self.part.at[theirs], self.cross, (p.e, p.column(0, True)))

    def cores(self):
        p, w, s = self.p, self.w, self.slots
        w.arrived(s[0], self.cross)
        far = lax.rem(p.x + 2, 4)

        def add(x):
            rows = self.at(p.c, x)
            theirs = pl.ds(pl.multiple_of(x * self.rows, self.rows), self.rows)
            mine = self.part[rows, :].astype(F32)
            self.part[rows, :] = (mine + self.cross[theirs, :].astype(F32)).astype(BF16)

        add(far)
        w.start(s[1], self.part.at[self.at(p.c, far, 0)], self.half.at[0], (p.e, p.column(1)))
        w.start(s[2], self.part.at[self.at(p.c, far, 1)], self.half.at[1], (p.e, p.column(-1)))
        add(lax.rem(p.x + 1, 4))
        add(lax.rem(p.x + 3, 4))
        add(p.x)

    def around(self):
        p, w, s = self.p, self.w, self.slots
        for side, step in ((0, 1), (1, -1)):
            x = lax.rem(p.x + step + 4, 4)
            w.arrived(s[1 + side], self.half.at[side])
            rows = self.at(p.c, x, side)
            mine = self.part[rows, :].astype(F32)
            self.part[rows, :] = (mine + self.half[side].astype(F32)).astype(BF16)
            w.start(
                s[3 + side], self.part.at[self.at(p.c, x)], self.full.at[side],
                (p.e, p.column(step)),
            )

    def settle(self):
        self.w.arrived(self.slots[3], self.full.at[0])
        self.w.arrived(self.slots[4], self.full.at[1])

    def value(self):
        total = self.part[self.at(self.p.c, self.p.x), :].astype(F32)
        return total + self.full[0].astype(F32) + self.full[1].astype(F32)

    def release(self):
        self.w.drain(self.slots)


class Exchange:
    def __init__(self, place, src, dst, send_sem, recv_sem, own_sem):
        self.p, self.src, self.dst = place, src, dst
        self.sems = (send_sem, recv_sem, own_sem)

    def begin(self):
        p = self.p
        send_sem, recv_sem, own_sem = self.sems
        for offset in PLANE:
            peer = p.plane(offset)
            pltpu.make_async_remote_copy(
                self.src.at[peer], self.dst.at[p.e], send_sem, recv_sem,
                device_id=(peer, p.t), device_id_type=MESH,
            ).start()
        pltpu.make_async_copy(self.src.at[p.e], self.dst.at[p.e], own_sem).start()

    def arrived(self):
        p = self.p
        others = self.dst.at[pl.ds(0, len(PLANE))]
        pltpu.make_async_copy(others, others, self.sems[1]).wait()
        pltpu.make_async_copy(self.src.at[p.e], self.dst.at[p.e], self.sems[2]).wait()

    def drain(self):
        others = self.src.at[pl.ds(0, len(PLANE))]
        pltpu.make_async_copy(others, others, self.sems[0]).wait()


def greet(place):
    barrier = pltpu.get_barrier_semaphore()
    count = 0
    for core in (False, True):
        for step in range(4):
            if step or core:
                dev = (place.e, place.column(step, core))
                pl.semaphore_signal(barrier, inc=1, device_id=dev, device_id_type=MESH)
                count += 1
    for offset in PLANE:
        dev = (place.plane(offset), place.t)
        pl.semaphore_signal(barrier, inc=1, device_id=dev, device_id_type=MESH)
        count += 1
    pl.semaphore_wait(barrier, count)


ORDER = (
    "ggB0", "P0", "ggB1", "ggF0", "saC0", "ggB2", "P1", "CH", "P2", "ggF1",
    "saC1", "P3", "ggF2", "ggE1", "saA0", "saC2", "ggE0", "SG1", "ggE2", "saA1",
    "saA2", "H0", "SG0", "P4", "SG2", "H1", "H2", "gnF0", "saC3", "P5",
    "gnF2", "gnE0", "saC4", "gnF1", "G0", "saA3", "SN0", "saC5", "saA4", "gnE2",
    "gnE1", "SN2", "H3", "saA5", "N0", "SN1", "gnF3", "H4", "G1", "N1",
    "gnE3", "H5", "R", "ggB3", "N2", "SN3", "gnF4", "G2", "gnF5", "N3",
    "ggB4", "gnE4", "RS", "ggB5", "gnE5", "ggF3", "SN4", "ggF4", "ggF5", "N4",
    "ggE3", "SN5", "N5", "ggE4", "SG3", "ggE5", "G3", "SG4", "SG5", "G4",
    "G5", "PARK", "FWD", "CT3", "O0", "CT2", "O1", "O2", "O3", "O4",
    "OS0", "CT4", "CT0", "OS1", "O5", "CT1", "CT5", "BH", "B0", "LO0",
    "PK", "B1", "LO1", "CO0", "CO1", "B2", "B3", "LB0", "soC1", "soC0",
    "CB0", "soA1", "B4", "sgC0", "soA0", "LB1", "CB1", "sgA0", "B5", "MX1",
    "sgC1", "LB2", "Q0", "CB2", "sgA1", "OS2", "OS3", "LB3", "sgC2", "grF0",
    "CB3", "Q1", "sgC3", "sgA2", "LB4", "sgA3", "Q2", "CB4", "LB5", "OS4",
    "Q3", "OS5", "CB5", "MX0", "grF1", "LO2", "grF2", "sgC4", "sgC5", "CO2",
    "grF3", "sgA4", "sgA5", "LO3", "grE1", "grE0", "soC2", "CO3", "Q4", "soC3",
    "soA2", "LO4", "CO4", "grE2", "grF4", "Q5", "LO5", "CO5", "AC0", "soC4",
    "soA3", "AC1", "soC5", "grE3", "grF5", "soA4", "grE4", "M", "AC2", "MX2",
    "AC3", "grE5", "soA5", "RES", "AC4", "MX4", "AC5", "MX3", "MX5", "END",
)


class Column:
    def __init__(self, ref, index, size):
        self.ref, self.index, self.size = ref, index, size

    def rows(self, key):
        if key is Ellipsis:
            return pl.ds(0, self.size)
        return key[0]

    def __getitem__(self, key):
        return self.ref[self.rows(key), self.index : self.index + 1]

    def __setitem__(self, key, value):
        self.ref[self.rows(key), self.index : self.index + 1] = value


def kernel(dims, *refs):
    tok, width, group, slots, inner = dims
    cuts = chunks_of(width)
    n = len(cuts)
    refs = list(refs)

    def take(k):
        out = refs[:k]
        del refs[:k]
        return out

    context, proj_t, res_t, gain, ids, counts, grad_t, up_t, down = take(9)
    mixed_t, residual_t, grad_context, park = take(4)
    land_g, land_o, land_b = take(n), take(n), take(n)
    rows_a, rows_b, rows_c = take(n), take(n), take(n)
    up, low = take(n), take(n)
    proj, hidden, info, pre, act, maps, cols = take(7)
    roots, root_out, root_in, slopes = take(4)
    part = take(n)
    cross_a, half_a, full_a = take(n), take(n), take(n)
    cross_b, half_b, full_b = take(n), take(n), take(n)
    send_sems, recv_sems, load_sems, plane_sems = refs

    p = Place()
    ctx = grad_context
    wire = Wire(send_sems, recv_sems)
    gather_g = [Gather(p, wire, up[j], tok) for j in range(n)]
    gather_n = [Gather(p, wire, low[j], tok) for j in range(n)]
    gather_r = [Gather(p, wire, up[j], tok) for j in range(n)]
    sum_a = [Scatter(p, wire, part[j], cross_a[j], half_a[j], full_a[j]) for j in range(n)]
    sum_o = [Scatter(p, wire, low[j], cross_b[j], half_b[j], full_b[j]) for j in range(n)]
    sum_g = [Scatter(p, wire, part[j], cross_a[j], half_a[j], full_a[j]) for j in range(n)]
    total, root_col, scale, square, cross = (
        Column(cols, i, size) for i, size in enumerate((8 * tok, 8 * tok, slots, tok, tok))
    )
    where = [(s, c) for c in (False, True) for s in range(4) if s or c]

    def everyone(table):
        reserved = [wire.reserve() for _ in where]

        def begin():
            for slot, (step, core) in zip(reserved, where):
                wire.start(slot, table.at[p.t], table.at[p.t], (p.e, p.column(step, core)))

        def settle():
            for slot, (step, core) in zip(reserved, where):
                wire.arrived(slot, table.at[p.column(-step, core)])

        return begin, settle

    info_begin, info_settle = everyone(info)
    roots_begin, roots_settle = everyone(roots)
    slopes_begin, slopes_settle = everyone(slopes)

    def exchanges(kind, src, dst):
        return [
            Exchange(p, src[j], dst[j], *(plane_sems.at[kind * n + j, i] for i in range(3)))
            for j in range(n)
        ]

    swap_g = exchanges(0, rows_a, land_g)
    swap_n = exchanges(1, rows_b, rows_c)
    swap_o = exchanges(2, rows_b, land_o)
    swap_b = exchanges(3, rows_c, land_b)
    swap_r = Exchange(p, root_out, root_in, *(plane_sems.at[4 * n, i] for i in range(3)))
    own_rows = pl.ds(pl.multiple_of(p.t * tok, tok), tok)

    def load(src, dst, j, kind):
        return pltpu.make_async_copy(src, dst, load_sems.at[j, kind])

    def row_block(index, size):
        return pl.ds(pl.multiple_of(index * size, size), size)

    span = 8 * group
    pair = 2 * tok
    depth = act.shape[2]
    tiles = inner // depth
    halves = range(slots // span)

    def peers(b):
        return pl.ds(b * 8, 8)

    def pre_rows(i, b):
        return pl.ds(pl.multiple_of(i * slots + b * span, span), span)

    def column(row):
        return jnp.broadcast_to(row, (tok, tok)).T[:, :1]

    def gain_of(j):
        at, w = cuts[j]
        return gain[at : at + w].astype(F32).reshape(1, w)

    def part_store(ref, quarter, at, size, value):
        ref[row_block(quarter, tok), at : at + size] = value[:tok]
        ref[row_block(4 + quarter, tok), at : at + size] = value[tok:]


    def begin_grads(j):
        gather_g[j].begin()

    def project(j):
        at_j, w = cuts[j]
        load(proj_t.at[pl.ds(at_j, w)], proj.at[pl.ds(at_j, w)], j, 0).wait()

        @pl.loop(0, 4)
        def _(quarter):
            lhs = ctx[row_block(quarter, pair), :]
            for at, size in tiles_of(w):
                got = dot_nt(lhs, proj[at_j + at : at_j + at + size, :]).astype(BF16)
                part_store(part[j], quarter, at, size, got)

        sum_a[j].begin()

    def choices():
        info_settle()

        @pl.loop(0, slots // 80)
        def _(block):
            first = block * 80 + p.t * slots
            slot_id = (lax.broadcasted_iota(jnp.int32, (80, tok), 0) + first).astype(F32)
            rows = row_block(block, 80)
            weight = jnp.zeros((80, tok), F32)
            for s in range(8):
                facts = info[s]
                whole = facts[4:5] + facts[5:6] + facts[6:7] + facts[7:8]
                hits = jnp.zeros((80, tok), F32)
                for k in range(4):
                    hit = slot_id == facts[k : k + 1]
                    hits = jnp.where(hit, 1.0, hits)
                    weight = jnp.where(hit, facts[4 + k : 5 + k] / whole, weight)
                maps[rows, s * tok : (s + 1) * tok] = hits.astype(BF16)
            scale[rows, :] = jnp.sum(weight, axis=1, keepdims=True)

    def select(j, table, out, weighted):
        @pl.loop(0, slots // span)
        def _(b):
            lhs = maps[row_block(b, span), : 8 * tok]
            for at, size in tiles_of(cuts[j][1]):
                rhs = table[: 8 * tok, at : at + size]
                got = jnp.dot(lhs, rhs, preferred_element_type=F32)
                if weighted:
                    got = got * scale[row_block(b, span), :]
                out[peers(b), :, at : at + size] = got.reshape(8, group, size).astype(BF16)

    def send_grads(j):
        gather_g[j].settle()
        select(j, up[j], rows_a[j], True)
        swap_g[j].begin()

    def project_back(j, table, first, scaled):
        at_j, w = cuts[j]

        @pl.loop(0, 4)
        def _(quarter):
            lhs = table[row_block(quarter, pair), :]
            if scaled:
                lhs = (lhs.astype(F32) * (1.0 / gain_of(j))).astype(BF16)
            value = jnp.dot(lhs, proj[at_j : at_j + w, :], preferred_element_type=F32)
            rows = row_block(first * 4 + quarter, pair)
            pre[rows, :] = value if j == 0 else pre[rows, :] + value

    def grads_back(j):
        project_back(j, up[j], 0, False)
        wire.drain(gather_g[j].slots)
        at, w = cuts[j]
        load(up_t.at[:, pl.ds(at, w)], up[j], j, 1).start()

    def hidden_chunk(j):
        at, w = cuts[j]
        sum_a[j].settle()
        value = res_t[at : at + w, :].astype(F32).T + sum_a[j].value()
        hidden[:, at : at + w] = value
        low[j][own_rows, :] = (value * gain_of(j)).astype(BF16)
        gather_n[j].begin()
        here = jnp.sum(value * value, axis=1, keepdims=True)
        square[...] = here if j == 0 else square[...] + here

    def root():
        inv = lax.rsqrt(square[...] / width + 1e-05)
        square[...] = inv
        roots[p.t] = jnp.broadcast_to(inv, (tok, tok)).T[:8]
        roots_begin()

    def send_roots():
        roots_settle()
        for s in range(8):
            root_col[s * tok : (s + 1) * tok, :] = column(roots[s][0:1])

        @pl.loop(0, slots // 80)
        def _(block):
            value = jnp.zeros((80, tok), F32)
            for s in range(8):
                hits = maps[row_block(block, 80), s * tok : (s + 1) * tok].astype(F32)
                value += hits * roots[s][0:1]
            value = jnp.sum(value, axis=1, keepdims=True)
            wide = jnp.broadcast_to(value, (80, tok)).reshape(80 // group, group, tok)
            root_out[pl.ds(block * (80 // group), 80 // group)] = wide

        swap_r.begin()

    def send_rows(j):
        gather_n[j].settle()
        select(j, low[j], rows_b[j], False)
        swap_n[j].begin()

    def rows_back(j):
        project_back(j, low[j], 1, True)
        wire.drain(gather_n[j].slots)
        at, w = cuts[j]
        load(down.at[:, pl.ds(at, w)], low[j], j, 2).start()

    def park_out():
        load(pre, park, n, 0).start()

    def picks():
        @pl.loop(0, 8)
        def _(s):
            facts = jnp.concatenate([info[s], jnp.zeros((tok - 8, tok), F32)], axis=0).T
            slot_id = (lax.broadcasted_iota(jnp.int32, (tok, slots), 1) + p.t * slots).astype(F32)
            hits = jnp.zeros((tok, slots), F32)
            taken = jnp.zeros((tok, slots), F32)
            for k in range(4):
                hit = slot_id == facts[:, k : k + 1]
                hits = jnp.where(hit, 1.0, hits)
                taken = jnp.where(hit, facts[:, 4 + k : 5 + k], taken)
            rows = row_block(s, tok)
            maps[rows, :slots] = hits.astype(BF16)
            maps[rows, slots:] = taken.astype(BF16)
            total[rows, :] = facts[:, 4:5] + facts[:, 5:6] + facts[:, 6:7] + facts[:, 7:8]

    def forward():
        load(pre, park, n, 0).wait()
        for j, (at, w) in enumerate(cuts):
            load(up_t.at[:, pl.ds(at, w)], up[j], j, 1).wait()
            swap_n[j].arrived()
            swap_n[j].drain()
        swap_r.arrived()
        swap_r.drain()

        @pl.loop(0, tiles)
        def _(i):
            @pl.loop(0, slots // span)
            def _(b):
                value = sum(
                    dot_nt(
                        rows_c[j][peers(b)].reshape(span, cuts[j][1]), up[j][row_block(i, depth), :]
                    )
                    for j in range(n)
                )
                value = value * root_in[peers(b)].reshape(span, tok)[:, :1]
                pre[pre_rows(i, b), :depth] = value
                act[i, row_block(b, span), :] = (value / (1.0 + jnp.exp(-value))).astype(BF16)

    def widen(weight, j, out):
        @pl.loop(0, slots // span)
        def _(b):
            for at, size in tiles_of(cuts[j][1]):
                value = sum(
                    jnp.dot(
                        act[i, row_block(b, span), :],
                        weight[j][i * depth : (i + 1) * depth, at : at + size],
                        preferred_element_type=F32,
                    )
                    for i in range(tiles)
                )
                out[peers(b), :, at : at + size] = value.reshape(8, group, size).astype(BF16)

    def expert_out(j):
        at, w = cuts[j]
        load(down.at[:, pl.ds(at, w)], low[j], j, 2).wait()
        widen(low, j, rows_b[j])

    def send_out(j):
        swap_o[j].begin()

    def take_grads(j):
        swap_g[j].arrived()
        swap_g[j].drain()
        load(land_g[j], rows_a[j], j, 3).start()

    def backward():
        for j in range(n):
            load(land_g[j], rows_a[j], j, 3).wait()

        @pl.loop(0, tiles)
        def _(i):
            @pl.loop(0, slots // span)
            def _(b):
                value = sum(
                    dot_nt(
                        rows_a[j][peers(b)].reshape(span, cuts[j][1]), low[j][row_block(i, depth), :]
                    )
                    for j in range(n)
                )
                before = pre[pre_rows(i, b), :depth]
                gate = 1.0 / (1.0 + jnp.exp(-before))
                slope = gate * (1.0 + before * (1.0 - gate))
                act[i, row_block(b, span), :] = (value * slope).astype(BF16)

        load(park, pre, n, 1).start()

    def expert_grad(j):
        widen(up, j, rows_c[j])
        swap_b[j].begin()

    def take_out(j):
        swap_o[j].arrived()
        load(land_o[j], rows_a[j], j, 4).start()

    def take_back(j):
        swap_b[j].arrived()
        load(land_b[j], rows_a[j], j, 5).start()

    def combine(j, first, rows, ref, shared):
        @pl.loop(0, 4)
        def _(quarter):
            lhs = maps[row_block(quarter, pair), first : first + slots]
            for at, size in tiles_of(cuts[j][1]):
                rhs = rows[:, :, at : at + size].reshape(slots, size)
                value = jnp.dot(lhs, rhs, preferred_element_type=F32)
                if shared:
                    value = value / total[row_block(quarter, pair), :]
                part_store(ref, quarter, at, size, value.astype(BF16))

    def mix_chunk(j):
        load(land_o[j], rows_a[j], j, 4).wait()
        combine(j, slots, rows_a[j], low[j], True)
        sum_o[j].begin()

    def grad_chunk(j):
        load(land_b[j], rows_a[j], j, 5).wait()
        sum_a[j].release()
        combine(j, 0, rows_a[j], part[j], False)
        sum_g[j].begin()

    def mixed_out(j):
        at, w = cuts[j]
        sum_o[j].settle()
        mixed_t[at : at + w, :] = (hidden[:, at : at + w] + sum_o[j].value()).T.astype(BF16)

    def scaled_grad(j):
        at, w = cuts[j]
        sum_g[j].settle()
        scaled = sum_g[j].value() * gain_of(j)
        up[j][own_rows, :] = scaled.astype(BF16)
        gather_r[j].begin()
        here = jnp.sum(hidden[:, at : at + w] * scaled, axis=1, keepdims=True)
        cross[...] = here if j == 0 else cross[...] + here

    def slope_out():
        inv = square[...]
        cross[...] = inv * inv * inv * (cross[...] / width)
        slopes[p.t] = jnp.broadcast_to(cross[...], (tok, tok)).T[:8]
        slopes_begin()

    def residual_out():
        for j, (at, w) in enumerate(cuts):
            scaled = sum_g[j].value() * gain_of(j)
            value = square[...] * scaled - hidden[:, at : at + w] * cross[...]
            residual_t[at : at + w, :] = (grad_t[at : at + w, :].astype(F32) + value.T).astype(BF16)

    def accumulate(j):
        if j == 0:
            load(park, pre, n, 1).wait()
        gather_r[j].settle()
        at, w = cuts[j]

        @pl.loop(0, 4)
        def _(quarter):
            rows = row_block(quarter, pair)
            value = jnp.dot(up[j][rows, :], proj[at : at + w, :], preferred_element_type=F32)
            pre[rows, :] = pre[rows, :] + value * root_col[rows, :]

    def context_out():
        slopes_settle()

        @pl.loop(0, 8)
        def _(s):
            rows = row_block(s, tok)
            value = pre[rows, :] - pre[row_block(8 + s, tok), :] * column(slopes[s][0:1])
            grad_context[rows, :] = value.astype(BF16)

    by_chunk = {"ggB": begin_grads, "P": project, "SG": send_grads, "G": grads_back}
    by_chunk |= {"H": hidden_chunk, "SN": send_rows, "N": rows_back, "O": expert_out}
    by_chunk |= {"CT": take_grads, "B": expert_grad, "LO": take_out, "LB": take_back}
    by_chunk |= {"CO": mix_chunk, "CB": grad_chunk, "MX": mixed_out, "Q": scaled_grad}
    by_chunk |= {"AC": accumulate, "OS": send_out}
    for name, gathers in (("gg", gather_g), ("gn", gather_n), ("gr", gather_r)):
        by_chunk[name + "F"] = lambda j, of=gathers: of[j].forward()
        by_chunk[name + "E"] = lambda j, of=gathers: of[j].finish()
    for name, sums in (("sa", sum_a), ("so", sum_o), ("sg", sum_g)):
        by_chunk[name + "C"] = lambda j, of=sums: of[j].cores()
        by_chunk[name + "A"] = lambda j, of=sums: of[j].around()
    once = {"CH": choices, "R": root, "RS": send_roots, "PK": picks, "PARK": park_out}
    once |= {"FWD": forward, "BH": backward, "M": slope_out, "RES": residual_out}
    once["END"] = context_out

    load(context, ctx, n, 2).start()
    for j, (at, w) in enumerate(cuts):
        load(proj_t.at[pl.ds(at, w)], proj.at[pl.ds(at, w)], j, 0).start()

    def own_grads(j):
        at, w = cuts[j]
        up[j][own_rows, :] = grad_t[at : at + w, :].astype(F32).T.astype(BF16)

    own_grads(0)
    greet(p)
    begin_grads(0)
    for j in range(1, n):
        own_grads(j)

    experts = 128
    which = lax.broadcasted_iota(jnp.int32, (experts, tok), 0)
    route = [ids[k : k + 1, :] for k in range(4)]
    named = sum((which == r).astype(F32) for r in route)
    before = (
        lax.broadcasted_iota(jnp.int32, (tok, tok), 0)
        < lax.broadcasted_iota(jnp.int32, (tok, tok), 1)
    ).astype(BF16)
    earlier = jnp.dot(named.astype(BF16), before, preferred_element_type=F32)
    codes = []
    for r in route:
        rank = jnp.sum(jnp.where(which == r, earlier, 0.0), axis=0, keepdims=True)
        place = jnp.bitwise_and(r, 7) * slots + jnp.right_shift(r, 3) * group + p.t * CAP
        codes.append(place.astype(F32) + rank)
    info[p.t] = jnp.concatenate(codes + [counts[...].astype(F32)], axis=0)
    info_begin()
    load(context, ctx, n, 2).wait()

    for step in ORDER[1:]:
        name = step.rstrip("0123456789")
        if name == step:
            once[name]()
        else:
            by_chunk[name](int(step[len(name) :]))

    for swapped in swap_o + swap_b:
        swapped.drain()
    wire.drain()


def whole_block(
    context, proj_t, res_t, gain, ids, counts, grad_t, up_t, down, n_expert, n_tensor
):
    width, tok = res_t.shape
    inner = down.shape[0]
    depth = proj_t.shape[1]
    group = n_tensor * CAP
    slots = n_expert * group
    cuts = chunks_of(width)
    n = len(cuts)
    tiles = 3
    hbm = pl.BlockSpec(memory_space=pl.ANY)
    vmem = pl.BlockSpec(memory_space=pltpu.VMEM)
    landing = [jax.ShapeDtypeStruct((n_expert, group, w), BF16) for _, w in cuts]
    per = lambda *lead: [pltpu.VMEM(lead + (w,), BF16) for _, w in cuts]
    small = pltpu.VMEM((n_tensor, 8, tok), F32)
    copies = (3 * 8 + 3 * 5) * n + 3 * 7
    work_rows = max(tiles * slots, 2 * n_tensor * tok)
    outs = pl.pallas_call(
        functools.partial(kernel, (tok, width, group, slots, inner)),
        out_shape=(
            jax.ShapeDtypeStruct((width, tok), BF16),
            jax.ShapeDtypeStruct((width, tok), BF16),
            jax.ShapeDtypeStruct((n_tensor * tok, depth), BF16),
            jax.ShapeDtypeStruct((work_rows, depth), F32),
            *landing * 3,
        ),
        in_specs=[hbm, hbm] + [vmem] * 5 + [hbm, hbm],
        out_specs=tuple([vmem] * 3 + [hbm] * (1 + 3 * n)),
        scratch_shapes=per(n_expert, group) * 3
        + per(inner) * 2
        + [
            pltpu.VMEM((width, depth), BF16),
            pltpu.VMEM((tok, width), F32),
            small,
            pltpu.VMEM((work_rows, depth), F32),
            pltpu.VMEM((tiles, slots, inner // tiles), BF16),
            pltpu.VMEM((n_tensor * tok, 2 * slots), BF16),
            pltpu.VMEM((n_tensor * tok, 128), F32),
            small,
            pltpu.VMEM((n_expert, group, tok), F32),
            pltpu.VMEM((n_expert, group, tok), F32),
            small,
        ]
        + per(n_tensor * tok)
        + (per(4 * tok) + per(2, tok // 2) + per(2, tok)) * 2
        + [
            pltpu.SemaphoreType.DMA((copies,)),
            pltpu.SemaphoreType.DMA((copies,)),
            pltpu.SemaphoreType.DMA((n + 1, 6)),
            pltpu.SemaphoreType.DMA((4 * n + 1, 3)),
        ],
        compiler_params=pltpu.CompilerParams(
            collective_id=1, has_side_effects=True, vmem_limit_bytes=VMEM_LIMIT
        ),
        name="whole_block",
    )(context, proj_t, res_t, gain, ids, counts, grad_t, up_t, down)
    return outs[0].T, outs[1].T, outs[2]


def local(
    context, out_proj, residual_in, gain, up_weight, down_weight, expert_ids, gate_counts, grad_out
):
    return whole_block(
        context, out_proj.T, residual_in.T, gain, expert_ids.T, gate_counts.T,
        grad_out.T, up_weight[0].T, down_weight[0], lax.axis_size("expert"), lax.axis_size("tensor"),
    )


def solution(mesh):
    whole = P(("expert", "tensor"), None)
    in_specs = (
        P("expert", "tensor"),
        P("tensor", None),
        whole,
        P(),
        P(("expert", "tensor"), None, None),
        P(("expert", "tensor"), None, None),
        whole,
        whole,
        whole,
    )
    out_specs = (whole, whole, P("expert", "tensor"))
    return jax.shard_map(local, mesh=mesh, in_specs=in_specs, out_specs=out_specs, check_vma=False)
```
